256 devices in a mesh: batch: 4 (over y_lo, core), marker: 8 (over z), space: 8 (over y_hi, x).
Axes of the slice: x: 4, y: 4 (y_hi: 2, y_lo: 2; y = y_hi * 2 + y_lo), z: 8, core: 2. Of those that a mesh axis runs over, the one named last changes fastest.
Arguments:
- tokens: bfloat16 [4, 512, 48, 512], P('batch', 'space', 'marker'), may hold values from -100 to 100, as said below
- gain_first: float32 [512], replicated, may hold values from 0.1 to 1.9
- w_qkv_space: bfloat16 [512, 1536], replicated, may hold values from -0.25 to 0.25
- w_out_space: bfloat16 [512, 512], replicated, may hold values from -0.25 to 0.25
- gain_second: float32 [512], replicated, may hold values from 0.1 to 1.9
- w_qkv_marker: bfloat16 [512, 1536], replicated, may hold values from -0.25 to 0.25
- w_out_marker: bfloat16 [512, 512], replicated, may hold values from -0.25 to 0.25
- upstream: bfloat16 [4, 512, 48, 512], P('batch', 'space', 'marker'), may hold values from -6 to 6
Outputs:
- d_tokens: bfloat16 [4, 512, 48, 512], P('batch', 'space', 'marker')
- g_qkv_space: float32 [512, 1536], P(('marker', 'space'))
- g_out_space: float32 [512, 512], P(('marker', 'space'))
- g_gain_first: float32 [512], P(('marker', 'space'))
- g_qkv_marker: float32 [512, 1536], P(('marker', 'space'))
- g_out_marker: float32 [512, 512], P(('marker', 'space'))
- g_gain_second: float32 [512], P(('marker', 'space'))
The draws below stay inside these ranges and needn't reach their ends.
Inputs may be any that keep to these rules, and one draw needn't show every extreme that they name: `tokens`: tokens have scales that differ from token to token and from feature to feature.
All inputs are finite; a program needn't handle non-finite values.
Results may differ from the reference program's by a relative error of at most 0.035.
Values may be sent and summed in bfloat16 or wider, within the bound.
No kernel may reach another device: no remote copies, remote signals or barrier semaphores. Data moves between devices by JAX's collectives and lax.ppermute only.
A program may use at most 128 MiB of HBM per device.

```python
import math
import jax
import jax.numpy as jnp
from jax import lax

D = 512
M = 48
HD = 64
P_SIZE = 512
CROPS = 4


def draw_tokens(key, part):
    key = jax.random.fold_in(key, 7)
    base_key, row_key, col_key = jax.random.split(key, 3)
    shape = (CROPS, P_SIZE, M, D)
    base = jax.random.normal(base_key, shape, jnp.float32)
    top = math.log(10.0)
    rows = jnp.exp(jax.random.uniform(row_key, (CROPS, P_SIZE, M, 1), jnp.float32, 0.0, top))
    columns = jnp.exp(jax.random.uniform(col_key, (D,), jnp.float32, 0.0, math.log(10.0)))
    value = jnp.clip(base, -5.0, 5.0) * rows * columns * 0.2
    return jnp.clip(value, -100.0, 100.0).astype(jnp.bfloat16)


def steps_of(own_key, shape, pieces, low, high):
    level, own = 1.0, jax.random.fold_in(own_key, 6)
    for axis_at, parts in pieces:
        heights = jnp.exp(jax.random.uniform(jax.random.fold_in(own, axis_at), (parts,), jnp.float32, low / len(pieces), high / len(pieces)))
        level = level * jnp.repeat(heights, shape[axis_at] // parts).reshape([-1 if axis == axis_at else 1 for axis in range(len(shape))])
    return level


def normal_values(own_key, extent, scale, limit, shards=(), kind=jnp.bfloat16):
    drawn = jax.random.normal(own_key, extent, jnp.float32) * scale
    if len(shards) > 0:
        drawn = steps_of(own_key, extent, shards, -0.22, 0.18) * drawn
    return jnp.clip(drawn, min=-limit, max=limit).astype(kind)


def setup_inputs(seed: int = 0) -> dict:
    key_of = jax.random.split(jax.random.key(seed), 9)
    return {
        "tokens": draw_tokens(jax.random.fold_in(key_of[8], 71), 0),
        "gain_first": jnp.clip(1.0 + 0.18 * jax.random.normal(key_of[1], (D,), jnp.float32), 0.1, 1.9),
        "w_qkv_space": normal_values(key_of[2], (D, 3 * D), D ** -0.5, 0.25),
        "w_out_space": normal_values(key_of[3], (D, D), D ** -0.5, 0.25),
        "gain_second": jnp.clip(1.0 + 0.18 * jax.random.normal(key_of[4], (D,), jnp.float32), 0.1, 1.9),
        "w_qkv_marker": normal_values(key_of[5], (D, 3 * D), D ** -0.5, 0.25),
        "w_out_marker": normal_values(key_of[6], (D, D), D ** -0.5, 0.25),
        "upstream": normal_values(key_of[7], (CROPS, P_SIZE, M, D), 1.0, 6.0, ((0, 4), (1, 8), (2, 8))),
    }


epsilon = 1e-06

def normalize(wide, gain):
    scale = lax.rsqrt(lax.optimization_barrier(jnp.mean(wide * wide, axis=-1, keepdims=True)) + epsilon)
    return wide * scale * gain

def unit_rows(values):
    scale = lax.rsqrt(lax.optimization_barrier(jnp.mean(values * values, axis=-1, keepdims=True)) + epsilon)
    return values * scale

def attend(packed):
    length = packed.shape[0]
    heads = packed.shape[-1] // (3 * HD)
    wide = packed.reshape(length, heads, 3, HD).astype(jnp.float32)
    query = unit_rows(wide[:, :, 0])
    keys = unit_rows(wide[:, :, 1])
    scores = jnp.einsum('qhe,khe->hqk', query, keys) / math.sqrt(HD)
    weights = jnp.exp(scores)
    weights = weights / lax.optimization_barrier(jnp.sum(weights, axis=-1, keepdims=True))
    rounded = lax.optimization_barrier(weights.astype(jnp.bfloat16)).astype(jnp.float32)
    mixed = jnp.einsum('hqk,khe->qhe', rounded, wide[:, :, 2])
    return mixed.reshape(length, heads * HD).astype(jnp.bfloat16)

def spatial(packed):
    moved = jnp.moveaxis(packed, 2, 0)
    result = lax.map(jax.checkpoint(jax.vmap(attend)), moved)
    return jnp.moveaxis(result, 0, 2)

def crosswise(packed):
    return lax.map(jax.checkpoint(jax.vmap(attend)), packed)

def outer_sum(left, right):
    dims = tuple(range(left.ndim - 1))
    return lax.dot_general(left, right, ((dims, dims), ((), ())), preferred_element_type=jnp.float32)

def backward_dot(values, weight):
    return lax.dot_general(values, weight, (((values.ndim - 1,), (1,)), ((), ())), preferred_element_type=jnp.float32)

def reference(tokens, gain_first, w_qkv_space, w_out_space, gain_second, w_qkv_marker, w_out_marker, upstream):
    wide_tokens = tokens.astype(jnp.float32)
    first_wide, first_back = jax.vjp(normalize, wide_tokens, gain_first)
    first = first_wide.astype(jnp.bfloat16)
    qkv_one = jnp.dot(first, w_qkv_space, preferred_element_type=jnp.float32).astype(jnp.bfloat16)
    heads_one, spatial_back = jax.vjp(spatial, qkv_one)
    middle = (wide_tokens + jnp.dot(heads_one, w_out_space, preferred_element_type=jnp.float32)).astype(jnp.bfloat16)
    second_wide, second_back = jax.vjp(normalize, middle.astype(jnp.float32), gain_second)
    second = second_wide.astype(jnp.bfloat16)
    qkv_two = jnp.dot(second, w_qkv_marker, preferred_element_type=jnp.float32).astype(jnp.bfloat16)
    heads_two, cross_back = jax.vjp(crosswise, qkv_two)
    d_heads_two = backward_dot(upstream, w_out_marker).astype(jnp.bfloat16)
    g_out_marker = outer_sum(heads_two, upstream)
    d_qkv_two = cross_back(d_heads_two)[0]
    g_qkv_marker = outer_sum(second, d_qkv_two)
    d_second = backward_dot(d_qkv_two, w_qkv_marker).astype(jnp.bfloat16)
    d_mid_norm, r_second = second_back(d_second.astype(jnp.float32))
    d_middle = (upstream.astype(jnp.float32) + d_mid_norm).astype(jnp.bfloat16)
    g_out_space = outer_sum(heads_one, d_middle)
    d_heads_one = backward_dot(d_middle, w_out_space).astype(jnp.bfloat16)
    d_qkv_one = spatial_back(d_heads_one)[0]
    g_qkv_space = outer_sum(first, d_qkv_one)
    d_first = backward_dot(d_qkv_one, w_qkv_space).astype(jnp.bfloat16)
    d_tok_norm, r_first = first_back(d_first.astype(jnp.float32))
    d_tokens = (d_middle.astype(jnp.float32) + d_tok_norm).astype(jnp.bfloat16)
    factor = 1.0 / math.sqrt(CROPS * P_SIZE * M)
    return (d_tokens, g_qkv_space * factor, g_out_space * factor, r_first * factor, g_qkv_marker * factor, g_out_marker * factor, r_second * factor)
```

```python
import functools
import math

import jax
import jax.numpy as jnp
from jax import lax
from jax.experimental import pallas as pl
from jax.experimental.pallas import tpu as pltpu
from jax.sharding import PartitionSpec as P

HD = 64
EPS = 1e-06
BF = jnp.bfloat16
F32 = jnp.float32
LOG2E = math.log2(math.e)
VMEM_LIMIT = 56 * 1024 * 1024


def low_half(rows, width=128):
    return lax.broadcasted_iota(jnp.int32, (rows, width), 1) % 128 < HD


def swap(x):
    return pltpu.roll(x, HD, 1)


def dot(a, b):
    return jnp.dot(a, b, preferred_element_type=F32)


def dot_nt(a, b):
    return lax.dot_general(a, b, (((1,), (1,)), ((), ())), preferred_element_type=F32)


def half_mean(x, lo):
    first = jnp.sum(jnp.where(lo, x, 0.0), axis=-1, keepdims=True)
    second = jnp.sum(jnp.where(lo, 0.0, x), axis=-1, keepdims=True)
    return jnp.where(lo, first, second) * (1.0 / HD)


def half_scale(x, lo):
    return lax.rsqrt(half_mean(x * x, lo) + EPS)


def only_half(x, unit):
    own = x[unit * HD : (unit + 1) * HD]
    zero = jnp.zeros_like(own)
    return jnp.concatenate([own, zero] if unit == 0 else [zero, own], axis=0)


def row_scale(x):
    return lax.rsqrt(jnp.mean(x * x, axis=-1, keepdims=True) + EPS)


def norm_back(x, gain, cotangent):
    scale = row_scale(x)
    unit = x * scale
    pulled = cotangent * gain
    return scale * (pulled - unit * jnp.mean(pulled * unit, axis=-1, keepdims=True))


def scaled_pair(query, keys, lo):
    q_scale = half_scale(query, lo)
    k_scale = half_scale(keys, lo)
    return query * q_scale, q_scale, keys * k_scale, k_scale


def pair_back(d_qn, d_kn, qn, q_scale, kn, k_scale, lo):
    d_q = q_scale * (d_qn - qn * half_mean(d_qn * qn, lo))
    d_k = k_scale * (d_kn - kn * half_mean(d_kn * kn, lo))
    return d_q, d_k


def project_kernel(tokens_ref, gain_ref, w_ref, first_ref, send_ref):
    lo = low_half(64)
    x = tokens_ref[...].astype(F32)
    first = (x * row_scale(x) * gain_ref[...]).astype(BF)
    first_ref[...] = first
    for hh in range(4):
        wide = dot(first, w_ref[:, hh * 384 : (hh + 1) * 384])
        for jj in range(3):
            a = wide[(2 * jj) * 64 : (2 * jj + 1) * 64]
            b = wide[(2 * jj + 1) * 64 : (2 * jj + 2) * 64]
            for block in range(3):
                ba = a[:, block * 128 : (block + 1) * 128]
                bb = b[:, block * 128 : (block + 1) * 128]
                left = jnp.where(lo, ba, swap(bb)).astype(BF)
                right = jnp.where(lo, swap(ba), bb).astype(BF)
                for half, value in ((0, left), (1, right)):
                    part = 2 * block + half
                    head, kind = 2 * hh + part // 3, part % 3
                    at = jj * 384 + kind * 128
                    send_ref[head, :, at : at + 128] = value


def spatial_kernel(qkv_ref, heads_ref, inv_ref):
    length = qkv_ref.shape[0]
    lo = low_half(length)
    step = 256
    for jj in range(3):
        at = jj * 384
        query = qkv_ref[:, at : at + 128].astype(F32)
        keys = qkv_ref[:, at + 128 : at + 256].astype(F32)
        values = qkv_ref[:, at + 256 : at + 384].astype(F32)
        qn, _, kn, _ = scaled_pair(query, keys, lo)
        q_t = (qn * (LOG2E / 8.0)).T.astype(BF)
        kb = kn.astype(BF)
        v_t = values.T.astype(BF)
        out = []
        for unit in range(2):
            q_own = only_half(q_t, unit)
            cols = []
            for start in range(0, length, step):
                e = jnp.exp2(dot(kb, q_own[:, start : start + step]))
                inv = 1.0 / jnp.sum(e, axis=0, keepdims=True)
                inv_ref[2 * jj + unit : 2 * jj + unit + 1, start : start + step] = inv
                cols.append(dot(v_t[unit * HD : (unit + 1) * HD], e.astype(BF)) * inv)
            out.append(jnp.concatenate(cols, axis=1))
        heads_ref[:, jj * 128 : (jj + 1) * 128] = jnp.concatenate(out, axis=0).T.astype(BF)


def spatial_back_kernel(qkv_ref, heads_ref, inv_ref, d_heads_ref, d_qkv_ref):
    length = qkv_ref.shape[0]
    lo = low_half(length)
    step = 256
    for jj in range(3):
        at = jj * 384
        query = qkv_ref[:, at : at + 128].astype(F32)
        keys = qkv_ref[:, at + 128 : at + 256].astype(F32)
        vb = qkv_ref[:, at + 256 : at + 384]
        qn, q_scale, kn, k_scale = scaled_pair(query, keys, lo)
        qs = qn * (LOG2E / 8.0)
        q_t = qs.T.astype(BF)
        qb = qs.astype(BF)
        kb = kn.astype(BF)
        k_t = kn.T.astype(BF)
        o_t = heads_ref[:, jj * 128 : (jj + 1) * 128].astype(F32).T
        g_t = d_heads_ref[:, jj * 128 : (jj + 1) * 128].astype(F32).T
        scaled, drops = [], []
        for unit in range(2):
            rows = slice(unit * HD, (unit + 1) * HD)
            own = g_t[rows] * inv_ref[2 * jj + unit : 2 * jj + unit + 1, :]
            scaled.append(own)
            drops.append(jnp.sum(own * o_t[rows], axis=0, keepdims=True))
        g_scaled = jnp.concatenate(scaled, axis=0)
        gb = g_scaled.T.astype(BF)
        g_scaled = g_scaled.astype(BF)
        d_q, d_k, d_v = [], [], []
        for unit in range(2):
            q_own = only_half(q_t, unit)
            g_own = only_half(g_scaled, unit)
            cols, dk, dv = [], 0.0, 0.0
            for start in range(0, length, step):
                part = slice(start, start + step)
                e = jnp.exp2(dot(kb, q_own[:, part]))
                ds = (e * (dot(vb, g_own[:, part]) - drops[unit][:, part])).astype(BF)
                cols.append(dot(k_t[unit * HD : (unit + 1) * HD], ds))
                dk = dk + dot(ds, qb[part])
                dv = dv + dot(e.astype(BF), gb[part])
            d_q.append(jnp.concatenate(cols, axis=1))
            d_k.append(dk)
            d_v.append(dv)
        d_qn = jnp.concatenate(d_q, axis=0).T * (1.0 / 8.0)
        d_kn = jnp.where(lo, d_k[0], d_k[1]) * (1.0 / LOG2E)
        dq, dk = pair_back(d_qn, d_kn, qn, q_scale, kn, k_scale, lo)
        d_qkv_ref[:, at : at + 128] = dq.astype(BF)
        d_qkv_ref[:, at + 128 : at + 256] = dk.astype(BF)
        d_qkv_ref[:, at + 256 : at + 384] = jnp.where(lo, d_v[0], d_v[1]).astype(BF)


def middle_kernel(
    got_ref, tokens_ref, up_ref, w_out_ref, gain_ref, w_qkv_ref, w_last_ref,
    heads_one_ref, second_ref, d_qkv_ref, heads_two_ref, d_middle_ref, send_ref,
    qkv_ref, d_two_ref,
):
    lo64 = low_half(64)
    for hh in range(4):
        for jj in range(3):
            a = got_ref[2 * hh, :, jj * 128 : (jj + 1) * 128].astype(F32)
            b = got_ref[2 * hh + 1, :, jj * 128 : (jj + 1) * 128].astype(F32)
            cols = slice(hh * 128, (hh + 1) * 128)
            heads_one_ref[(2 * jj) * 64 : (2 * jj + 1) * 64, cols] = jnp.where(lo64, a, swap(b)).astype(BF)
            heads_one_ref[(2 * jj + 1) * 64 : (2 * jj + 2) * 64, cols] = jnp.where(lo64, swap(a), b).astype(BF)
    middle = tokens_ref[...].astype(F32) + dot(heads_one_ref[...], w_out_ref[...])
    middle = middle.astype(BF).astype(F32)
    gain = gain_ref[...]
    second = (middle * row_scale(middle) * gain).astype(BF)
    second_ref[...] = second
    qkv_ref[...] = dot(second, w_qkv_ref[...]).astype(BF)
    d_two_ref[...] = dot_nt(up_ref[...], w_last_ref[...]).astype(BF)

    length = qkv_ref.shape[0]
    lo = low_half(length)
    same = (
        lax.broadcasted_iota(jnp.int32, (length, length), 0) % 8
        == lax.broadcasted_iota(jnp.int32, (length, length), 1) % 8
    )
    for hh in range(4):
        at = hh * 384
        b0 = qkv_ref[:, at : at + 128].astype(F32)
        b1 = qkv_ref[:, at + 128 : at + 256].astype(F32)
        b2 = qkv_ref[:, at + 256 : at + 384].astype(F32)
        query = jnp.where(lo, b0, b1)
        keys = swap(jnp.where(lo, b2, b0))
        values = jnp.where(lo, b1, b2)
        qn, q_scale, kn, k_scale = scaled_pair(query, keys, lo)
        qs = qn * (LOG2E / 8.0)
        q_t = qs.T.astype(BF)
        qb = qs.astype(BF)
        kb = kn.astype(BF)
        k_t = kn.T.astype(BF)
        vb = values.astype(BF)
        v_t = values.T.astype(BF)
        g_t = d_two_ref[:, hh * 128 : (hh + 1) * 128].astype(F32).T
        o_t, d_q, d_k, d_v = [], [], [], []
        for unit in range(2):
            rows = slice(unit * HD, (unit + 1) * HD)
            e = jnp.where(same, jnp.exp2(dot(kb, only_half(q_t, unit))), 0.0)
            inv = 1.0 / jnp.sum(e, axis=0, keepdims=True)
            eb = e.astype(BF)
            o = dot(v_t[rows], eb) * inv
            own = g_t[rows] * inv
            drop = jnp.sum(own * o, axis=0, keepdims=True)
            zero = jnp.zeros_like(own)
            g_own = jnp.concatenate([own, zero] if unit == 0 else [zero, own], axis=0)
            gb = g_own.T.astype(BF)
            ds = (e * (dot(vb, g_own.astype(BF)) - drop)).astype(BF)
            o_t.append(o)
            d_q.append(dot(k_t[rows], ds))
            d_k.append(dot(ds, qb))
            d_v.append(dot(eb, gb))
        heads_two_ref[:, hh * 128 : (hh + 1) * 128] = jnp.concatenate(o_t, axis=0).T.astype(BF)
        d_qn = jnp.concatenate(d_q, axis=0).T * (1.0 / 8.0)
        d_kn = jnp.where(lo, d_k[0], d_k[1]) * (1.0 / LOG2E)
        dq, dk = pair_back(d_qn, d_kn, qn, q_scale, kn, k_scale, lo)
        dv = jnp.where(lo, d_v[0], d_v[1])
        dk = swap(dk)
        d_qkv_ref[:, at : at + 128] = jnp.where(lo, dq, dk).astype(BF)
        d_qkv_ref[:, at + 128 : at + 256] = jnp.where(lo, dv, dq).astype(BF)
        d_qkv_ref[:, at + 256 : at + 384] = jnp.where(lo, dk, dv).astype(BF)

    d_second = dot_nt(d_qkv_ref[...], w_qkv_ref[...]).astype(BF).astype(F32)
    d_middle = (up_ref[...].astype(F32) + norm_back(middle, gain, d_second)).astype(BF)
    d_middle_ref[...] = d_middle
    d_heads = dot_nt(d_middle, w_out_ref[...])
    for hh in range(4):
        for jj in range(3):
            a = d_heads[(2 * jj) * 64 : (2 * jj + 1) * 64, hh * 128 : (hh + 1) * 128]
            b = d_heads[(2 * jj + 1) * 64 : (2 * jj + 2) * 64, hh * 128 : (hh + 1) * 128]
            cols = slice(jj * 128, (jj + 1) * 128)
            send_ref[2 * hh, :, cols] = jnp.where(lo64, a, swap(b)).astype(BF)
            send_ref[2 * hh + 1, :, cols] = jnp.where(lo64, swap(a), b).astype(BF)


def last_kernel(got_ref, w_ref, tokens_ref, gain_ref, d_middle_ref, out_ref, d_qkv_ref):
    lo = low_half(64)
    for hh in range(4):
        for jj in range(3):
            part = []
            for head in (2 * hh, 2 * hh + 1):
                for kind in range(3):
                    at = jj * 384 + kind * 128
                    part.append(got_ref[head, :, at : at + 128].astype(F32))
            for block in range(3):
                left, right = part[2 * block], part[2 * block + 1]
                at = hh * 384 + block * 128
                d_qkv_ref[(2 * jj) * 64 : (2 * jj + 1) * 64, at : at + 128] = jnp.where(
                    lo, left, swap(right)
                ).astype(BF)
                d_qkv_ref[(2 * jj + 1) * 64 : (2 * jj + 2) * 64, at : at + 128] = jnp.where(
                    lo, swap(left), right
                ).astype(BF)
    d_first = dot_nt(d_qkv_ref[...], w_ref[...]).astype(BF).astype(F32)
    x = tokens_ref[...].astype(F32)
    out_ref[...] = (
        d_middle_ref[...].astype(F32) + norm_back(x, gain_ref[...], d_first)
    ).astype(BF)


def column_kernel(first_ref, d_qkv_ref, out_ref):
    lo = low_half(64, 384)
    total = jnp.zeros((512, 384), F32)
    for s in range(8):
        rows = []
        for jj in range(3):
            block = d_qkv_ref[s * 64 : (s + 1) * 64, jj * 384 : (jj + 1) * 384].astype(F32)
            rows.append(jnp.where(lo, block, 0.0).astype(BF))
            rows.append(jnp.where(lo, 0.0, block).astype(BF))
        total = total + dot(first_ref[s], jnp.concatenate(rows, axis=0))
    low = low_half(512)
    sums = [total[:, i * 128 : (i + 1) * 128] for i in range(3)]
    sums = [x + swap(x) for x in sums]
    out_ref[:, 0:128] = jnp.where(low, sums[0], sums[1]).astype(BF)
    out_ref[:, 128:192] = sums[2][:, :HD].astype(BF)


def call(kernel, outs, args, scratch=(), flops=10**9, moved=4 * 10**6, exps=0):
    return pl.pallas_call(
        kernel,
        out_shape=[jax.ShapeDtypeStruct(shape, dtype) for shape, dtype in outs],
        scratch_shapes=list(scratch),
        compiler_params=pltpu.CompilerParams(vmem_limit_bytes=VMEM_LIMIT),
        cost_estimate=pl.CostEstimate(flops=flops, bytes_accessed=moved, transcendentals=exps),
    )(*args)


def outer(left, right):
    return lax.dot_general(
        left, right, (((0,), (0,)), ((), ())), preferred_element_type=F32
    ).astype(BF)


def to_markers(x):
    lead = x.shape[:-2]
    k = len(lead)
    x = x.reshape(*lead, 6, 8, 8, 512)
    order = (k + 1, *range(k), k, k + 2, k + 3)
    x = jnp.transpose(x, order)
    x = lax.all_to_all(x, "marker", 0, 0, tiled=True)
    back = [0] * len(order)
    for i, o in enumerate(order):
        back[o] = i
    return jnp.transpose(x, back).reshape(*lead, 384, 512)


def swapped(x, bit):
    n = lax.axis_size("batch")
    return lax.ppermute(x, "batch", [(i, i ^ bit) for i in range(n)])


def halve(x, bit, shift):
    width = x.shape[1] // 2
    mine = (lax.axis_index("batch") >> shift) & 1
    keep = lax.dynamic_slice_in_dim(x, mine * width, width, 1)
    give = lax.dynamic_slice_in_dim(x, (1 - mine) * width, width, 1)
    return (keep.astype(F32) + swapped(give, bit).astype(F32)).astype(BF)


def on_device(
    tokens, gain_first, w_qkv_space, w_out_space, gain_second, w_qkv_marker, w_out_marker, upstream
):
    both = ("space", "marker")
    rows = ("marker", "space")
    mine = jnp.transpose(tokens[0], (1, 0, 2)).reshape(384, 512)
    up_mine = jnp.transpose(upstream[0], (1, 0, 2)).reshape(384, 512)
    gain_1 = gain_first.reshape(1, 512)
    gain_2 = gain_second.reshape(1, 512)

    first, qkv_send = call(
        project_kernel,
        [((384, 512), BF), ((8, 64, 1152), BF)],
        (mine, gain_1, w_qkv_space),
    )
    qkv_one = lax.all_to_all(qkv_send, "space", 0, 0, tiled=True).reshape(512, 1152)
    wide = to_markers(jnp.stack([mine, up_mine]))
    first_all = lax.all_gather(first.T, "space", axis=0, tiled=False)

    heads, inv = call(
        spatial_kernel, [((512, 384), BF), ((6, 512), F32)], (qkv_one,),
        flops=2 * 10**9, exps=6 * 512 * 512,
    )
    got = lax.all_to_all(heads, both, 0, 0, tiled=True).reshape(8, 64, 384)

    up_all = wide[1]
    heads_one, second, d_qkv_two, heads_two, d_middle, d_send = call(
        middle_kernel,
        [((384, 512), BF), ((384, 512), BF), ((384, 1536), BF), ((384, 512), BF),
         ((384, 512), BF), ((8, 64, 384), BF)],
        (got, wide[0], up_all, w_out_space, gain_2, w_qkv_marker, w_out_marker),
        scratch=[pltpu.VMEM((384, 1536), BF), pltpu.VMEM((384, 512), BF)],
        flops=6 * 10**9, exps=8 * 384 * 384,
    )
    d_heads = lax.all_to_all(d_send.reshape(512, 384), both, 0, 0, tiled=True)
    d_middle_mine = to_markers(d_middle)

    d_qkv_one, = call(
        spatial_back_kernel, [((512, 1152), BF)], (qkv_one, heads, inv, d_heads),
        flops=5 * 10**9, exps=6 * 512 * 512,
    )
    d_back = lax.all_to_all(d_qkv_one, "space", 0, 0, tiled=True).reshape(8, 64, 1152)
    d_tokens, = call(
        last_kernel, [((384, 512), BF)], (d_back, w_qkv_space, mine, gain_1, d_middle_mine),
        scratch=[pltpu.VMEM((384, 1536), BF)],
    )

    grads = jnp.concatenate(
        [outer(second, d_qkv_two), outer(heads_one, d_middle), outer(heads_two, up_all)], axis=1
    )
    share = halve(halve(grads, 1, 0), 2, 1)
    share = lax.all_to_all(share, rows, 0, 0, tiled=True)
    share = jnp.sum(share.reshape(64, 8, 640).astype(F32), axis=0).astype(BF)
    share = lax.all_gather(share, "batch", axis=0, tiled=False)
    share = share.reshape(2, 2, 8, 640).transpose(2, 1, 0, 3).reshape(8, 2560).astype(F32)

    column, = call(column_kernel, [((512, 192), BF)], (first_all, d_qkv_one), flops=2 * 10**9)
    column = lax.all_to_all(column, rows, 0, 0, tiled=True)
    column = jnp.sum(column.reshape(8, 8, 8, 192).astype(F32), axis=0)
    column = column.transpose(1, 0, 2).reshape(8, 1536).astype(BF)
    column = lax.all_gather(column, "batch", axis=0, tiled=False)
    column = jnp.sum(column.astype(F32), axis=0)

    count = 1
    for axis in ("batch", "marker", "space"):
        count *= lax.axis_size(axis)
    factor = 1.0 / math.sqrt(count * 384)
    at = (lax.axis_index("marker") * 8 + lax.axis_index("space")) * 8

    def gain_grad(weight, gain, grad):
        w = lax.dynamic_slice_in_dim(weight, at, 8, 0).astype(F32)
        return jnp.sum(w * grad, axis=1) / lax.dynamic_slice_in_dim(gain, at, 8, 0)

    g_qkv_space = column * factor
    g_qkv_marker = share[:, :1536] * factor
    return (
        jnp.transpose(d_tokens.reshape(6, 64, 512), (1, 0, 2))[None],
        g_qkv_space,
        share[:, 1536:2048] * factor,
        gain_grad(w_qkv_space, gain_first, g_qkv_space),
        g_qkv_marker,
        share[:, 2048:] * factor,
        gain_grad(w_qkv_marker, gain_second, g_qkv_marker),
    )


def solution(mesh):
    in_specs = (
        P("batch", "space", "marker", None),
        P(), P(), P(), P(), P(), P(),
        P("batch", "space", "marker", None),
    )
    shares = P(("marker", "space"), None)
    out_specs = (
        P("batch", "space", "marker", None),
        shares,
        shares,
        P(("marker", "space")),
        shares,
        shares,
        P(("marker", "space")),
    )
    return jax.shard_map(
        on_device, mesh=mesh, in_specs=in_specs, out_specs=out_specs, check_vma=False
    )
```

```python
import functools
import math

import jax
import jax.numpy as jnp
from jax import lax
from jax.experimental import pallas as pl
from jax.experimental.pallas import tpu as pltpu
from jax.sharding import PartitionSpec as P

HD = 64
EPS = 1e-06
BF = jnp.bfloat16
F32 = jnp.float32
LOG2E = math.log2(math.e)
SMALL = 24 * 1024 * 1024
LARGE = 56 * 1024 * 1024


def low_half(rows, width=128):
    return lax.broadcasted_iota(jnp.int32, (rows, width), 1) % 128 < HD


def swap(x):
    return pltpu.roll(x, HD, 1)


def dot(a, b):
    return jnp.dot(a, b, preferred_element_type=F32)


def dot_nt(a, b):
    return lax.dot_general(a, b, (((1,), (1,)), ((), ())), preferred_element_type=F32)


def outer(left, right):
    return lax.dot_general(
        left, right, (((0,), (0,)), ((), ())), preferred_element_type=F32
    ).astype(BF)


def half_mean(x, lo):
    first = jnp.sum(jnp.where(lo, x, 0.0), axis=-1, keepdims=True)
    second = jnp.sum(jnp.where(lo, 0.0, x), axis=-1, keepdims=True)
    return jnp.where(lo, first, second) * (1.0 / HD)


def half_scale(x, lo):
    return lax.rsqrt(half_mean(x * x, lo) + EPS)


def only_half(x, unit):
    own = x[unit * HD : (unit + 1) * HD]
    zero = jnp.zeros_like(own)
    return jnp.concatenate([own, zero] if unit == 0 else [zero, own], axis=0)


def row_scale(x):
    return lax.rsqrt(jnp.mean(x * x, axis=-1, keepdims=True) + EPS)


def norm_back(x, gain, cotangent):
    scale = row_scale(x)
    unit = x * scale
    pulled = cotangent * gain
    return scale * (pulled - unit * jnp.mean(pulled * unit, axis=-1, keepdims=True))


def scaled_pair(query, keys, lo):
    q_scale = half_scale(query, lo)
    k_scale = half_scale(keys, lo)
    return query * q_scale, q_scale, keys * k_scale, k_scale


def pair_back(d_qn, d_kn, qn, q_scale, kn, k_scale, lo):
    d_q = q_scale * (d_qn - qn * half_mean(d_qn * qn, lo))
    d_k = k_scale * (d_kn - kn * half_mean(d_kn * kn, lo))
    return d_q, d_k


def project_kernel(tokens_ref, gain_ref, w_ref, first_t_ref, send_ref):
    lo = low_half(64)
    x = tokens_ref[...].astype(F32)
    first = (x * row_scale(x) * gain_ref[...]).astype(BF)
    first_t_ref[...] = first.astype(F32).T.astype(BF)
    for hh in range(4):
        wide = dot(first, w_ref[:, hh * 384 : (hh + 1) * 384])
        for jj in range(3):
            a = wide[(2 * jj) * 64 : (2 * jj + 1) * 64]
            b = wide[(2 * jj + 1) * 64 : (2 * jj + 2) * 64]
            for block in range(3):
                ba = a[:, block * 128 : (block + 1) * 128]
                bb = b[:, block * 128 : (block + 1) * 128]
                left = jnp.where(lo, ba, swap(bb)).astype(BF)
                right = jnp.where(lo, swap(ba), bb).astype(BF)
                for half, value in ((0, left), (1, right)):
                    part = 2 * block + half
                    head, kind = 2 * hh + part // 3, part % 3
                    at = jj * 384 + kind * 128
                    send_ref[head, :, at : at + 128] = value


def spatial_kernel(qkv_ref, heads_ref, inv_ref):
    length = qkv_ref.shape[0]
    lo = low_half(length)
    step = 256
    for jj in range(3):
        at = jj * 384
        query = qkv_ref[:, at : at + 128].astype(F32)
        keys = qkv_ref[:, at + 128 : at + 256].astype(F32)
        values = qkv_ref[:, at + 256 : at + 384].astype(F32)
        qn, _, kn, _ = scaled_pair(query, keys, lo)
        q_t = (qn * (LOG2E / 8.0)).T.astype(BF)
        kb = kn.astype(BF)
        v_t = values.T.astype(BF)
        out = []
        for unit in range(2):
            q_own = only_half(q_t, unit)
            cols = []
            for start in range(0, length, step):
                e = jnp.exp2(dot(kb, q_own[:, start : start + step]))
                inv = 1.0 / jnp.sum(e, axis=0, keepdims=True)
                inv_ref[2 * jj + unit : 2 * jj + unit + 1, start : start + step] = inv
                cols.append(dot(v_t[unit * HD : (unit + 1) * HD], e.astype(BF)) * inv)
            out.append(jnp.concatenate(cols, axis=1))
        heads_ref[:, jj * 128 : (jj + 1) * 128] = jnp.concatenate(out, axis=0).T.astype(BF)


def spatial_back_kernel(qkv_ref, heads_ref, inv_ref, d_heads_ref, d_qkv_ref):
    length = qkv_ref.shape[0]
    lo = low_half(length)
    step = 256
    for jj in range(3):
        at = jj * 384
        query = qkv_ref[:, at : at + 128].astype(F32)
        keys = qkv_ref[:, at + 128 : at + 256].astype(F32)
        vb = qkv_ref[:, at + 256 : at + 384]
        qn, q_scale, kn, k_scale = scaled_pair(query, keys, lo)
        qs = qn * (LOG2E / 8.0)
        q_t = qs.T.astype(BF)
        qb = qs.astype(BF)
        kb = kn.astype(BF)
        k_t = kn.T.astype(BF)
        o_t = heads_ref[:, jj * 128 : (jj + 1) * 128].astype(F32).T
        g_t = d_heads_ref[:, jj * 128 : (jj + 1) * 128].astype(F32).T
        scaled, drops = [], []
        for unit in range(2):
            rows = slice(unit * HD, (unit + 1) * HD)
            own = g_t[rows] * inv_ref[2 * jj + unit : 2 * jj + unit + 1, :]
            scaled.append(own)
            drops.append(jnp.sum(own * o_t[rows], axis=0, keepdims=True))
        g_scaled = jnp.concatenate(scaled, axis=0)
        gb = g_scaled.T.astype(BF)
        g_scaled = g_scaled.astype(BF)
        d_q, d_k, d_v = [], [], []
        for unit in range(2):
            q_own = only_half(q_t, unit)
            g_own = only_half(g_scaled, unit)
            cols, dk, dv = [], 0.0, 0.0
            for start in range(0, length, step):
                part = slice(start, start + step)
                e = jnp.exp2(dot(kb, q_own[:, part]))
                ds = (e * (dot(vb, g_own[:, part]) - drops[unit][:, part])).astype(BF)
                cols.append(dot(k_t[unit * HD : (unit + 1) * HD], ds))
                dk = dk + dot(ds, qb[part])
                dv = dv + dot(e.astype(BF), gb[part])
            d_q.append(jnp.concatenate(cols, axis=1))
            d_k.append(dk)
            d_v.append(dv)
        d_qn = jnp.concatenate(d_q, axis=0).T * (1.0 / 8.0)
        d_kn = jnp.where(lo, d_k[0], d_k[1]) * (1.0 / LOG2E)
        dq, dk = pair_back(d_qn, d_kn, qn, q_scale, kn, k_scale, lo)
        d_qkv_ref[:, at : at + 128] = dq.astype(BF)
        d_qkv_ref[:, at + 128 : at + 256] = dk.astype(BF)
        d_qkv_ref[:, at + 256 : at + 384] = jnp.where(lo, d_v[0], d_v[1]).astype(BF)


def middle_kernel(
    core_ref, got_ref, tokens_ref, up_ref, w_out_ref, gain_ref, w_qkv_ref, w_last_ref,
    keep_ref, give_ref, d_middle_ref, send_ref,
    grads_ref, heads_one_ref, second_ref, d_qkv_ref, heads_two_ref, qkv_ref, d_two_ref,
):
    lo64 = low_half(64)
    for hh in range(4):
        for jj in range(3):
            a = got_ref[2 * hh, :, jj * 128 : (jj + 1) * 128].astype(F32)
            b = got_ref[2 * hh + 1, :, jj * 128 : (jj + 1) * 128].astype(F32)
            cols = slice(hh * 128, (hh + 1) * 128)
            heads_one_ref[(2 * jj) * 64 : (2 * jj + 1) * 64, cols] = jnp.where(lo64, a, swap(b)).astype(BF)
            heads_one_ref[(2 * jj + 1) * 64 : (2 * jj + 2) * 64, cols] = jnp.where(lo64, swap(a), b).astype(BF)
    middle = tokens_ref[...].astype(F32) + dot(heads_one_ref[...], w_out_ref[...])
    middle = middle.astype(BF).astype(F32)
    gain = gain_ref[...]
    second = (middle * row_scale(middle) * gain).astype(BF)
    second_ref[...] = second
    qkv_ref[...] = dot(second, w_qkv_ref[...]).astype(BF)
    d_two_ref[...] = dot_nt(up_ref[...], w_last_ref[...]).astype(BF)

    length = qkv_ref.shape[0]
    lo = low_half(length)
    same = (
        lax.broadcasted_iota(jnp.int32, (length, length), 0) % 8
        == lax.broadcasted_iota(jnp.int32, (length, length), 1) % 8
    )
    for hh in range(4):
        at = hh * 384
        b0 = qkv_ref[:, at : at + 128].astype(F32)
        b1 = qkv_ref[:, at + 128 : at + 256].astype(F32)
        b2 = qkv_ref[:, at + 256 : at + 384].astype(F32)
        query = jnp.where(lo, b0, b1)
        keys = swap(jnp.where(lo, b2, b0))
        values = jnp.where(lo, b1, b2)
        qn, q_scale, kn, k_scale = scaled_pair(query, keys, lo)
        qs = qn * (LOG2E / 8.0)
        q_t = qs.T.astype(BF)
        qb = qs.astype(BF)
        kb = kn.astype(BF)
        k_t = kn.T.astype(BF)
        vb = values.astype(BF)
        v_t = values.T.astype(BF)
        g_t = d_two_ref[:, hh * 128 : (hh + 1) * 128].astype(F32).T
        o_t, d_q, d_k, d_v = [], [], [], []
        for unit in range(2):
            rows = slice(unit * HD, (unit + 1) * HD)
            e = jnp.where(same, jnp.exp2(dot(kb, only_half(q_t, unit))), 0.0)
            inv = 1.0 / jnp.sum(e, axis=0, keepdims=True)
            eb = e.astype(BF)
            o = dot(v_t[rows], eb) * inv
            own = g_t[rows] * inv
            drop = jnp.sum(own * o, axis=0, keepdims=True)
            zero = jnp.zeros_like(own)
            g_own = jnp.concatenate([own, zero] if unit == 0 else [zero, own], axis=0)
            gb = g_own.T.astype(BF)
            ds = (e * (dot(vb, g_own.astype(BF)) - drop)).astype(BF)
            o_t.append(o)
            d_q.append(dot(k_t[rows], ds))
            d_k.append(dot(ds, qb))
            d_v.append(dot(eb, gb))
        heads_two_ref[:, hh * 128 : (hh + 1) * 128] = jnp.concatenate(o_t, axis=0).T.astype(BF)
        d_qn = jnp.concatenate(d_q, axis=0).T * (1.0 / 8.0)
        d_kn = jnp.where(lo, d_k[0], d_k[1]) * (1.0 / LOG2E)
        dq, dk = pair_back(d_qn, d_kn, qn, q_scale, kn, k_scale, lo)
        dv = jnp.where(lo, d_v[0], d_v[1])
        dk = swap(dk)
        d_qkv_ref[:, at : at + 128] = jnp.where(lo, dq, dk).astype(BF)
        d_qkv_ref[:, at + 128 : at + 256] = jnp.where(lo, dv, dq).astype(BF)
        d_qkv_ref[:, at + 256 : at + 384] = jnp.where(lo, dk, dv).astype(BF)

    d_second = dot_nt(d_qkv_ref[...], w_qkv_ref[...]).astype(BF).astype(F32)
    d_middle = (up_ref[...].astype(F32) + norm_back(middle, gain, d_second)).astype(BF)
    d_middle_ref[...] = d_middle
    d_heads = dot_nt(d_middle, w_out_ref[...])
    for hh in range(4):
        for jj in range(3):
            a = d_heads[(2 * jj) * 64 : (2 * jj + 1) * 64, hh * 128 : (hh + 1) * 128]
            b = d_heads[(2 * jj + 1) * 64 : (2 * jj + 2) * 64, hh * 128 : (hh + 1) * 128]
            cols = slice(jj * 128, (jj + 1) * 128)
            send_ref[2 * hh, :, cols] = jnp.where(lo64, a, swap(b)).astype(BF)
            send_ref[2 * hh + 1, :, cols] = jnp.where(lo64, swap(a), b).astype(BF)
    grads_ref[:, :1536] = outer(second_ref[...], d_qkv_ref[...])
    grads_ref[:, 1536:2048] = outer(heads_one_ref[...], d_middle)
    grads_ref[:, 2048:] = outer(heads_two_ref[...], up_ref[...])
    core = core_ref[0]
    keep_ref[...] = grads_ref[:, pl.ds(pl.multiple_of(core * 1280, 1280), 1280)]
    give_ref[...] = grads_ref[:, pl.ds(pl.multiple_of((1 - core) * 1280, 1280), 1280)]


def last_kernel(got_ref, w_ref, tokens_ref, gain_ref, d_middle_ref, out_ref, d_qkv_ref):
    lo = low_half(64)
    for hh in range(4):
        for jj in range(3):
            part = []
            for head in (2 * hh, 2 * hh + 1):
                for kind in range(3):
                    at = jj * 384 + kind * 128
                    part.append(got_ref[head, :, at : at + 128].astype(F32))
            for block in range(3):
                left, right = part[2 * block], part[2 * block + 1]
                at = hh * 384 + block * 128
                d_qkv_ref[(2 * jj) * 64 : (2 * jj + 1) * 64, at : at + 128] = jnp.where(
                    lo, left, swap(right)
                ).astype(BF)
                d_qkv_ref[(2 * jj + 1) * 64 : (2 * jj + 2) * 64, at : at + 128] = jnp.where(
                    lo, swap(left), right
                ).astype(BF)
    d_first = dot_nt(d_qkv_ref[...], w_ref[...]).astype(BF).astype(F32)
    x = tokens_ref[...].astype(F32)
    out_ref[...] = (
        d_middle_ref[...].astype(F32) + norm_back(x, gain_ref[...], d_first)
    ).astype(BF)


def column_kernel(first_ref, d_qkv_ref, out_ref):
    lo = low_half(64, 384)
    total = jnp.zeros((512, 384), F32)
    for s in range(8):
        rows = []
        for jj in range(3):
            block = d_qkv_ref[s * 64 : (s + 1) * 64, jj * 384 : (jj + 1) * 384].astype(F32)
            rows.append(jnp.where(lo, block, 0.0).astype(BF))
            rows.append(jnp.where(lo, 0.0, block).astype(BF))
        total = total + dot(first_ref[s], jnp.concatenate(rows, axis=0))
    low = low_half(512)
    sums = [total[:, i * 128 : (i + 1) * 128] for i in range(3)]
    sums = [x + swap(x) for x in sums]
    out_ref[:, 0:128] = jnp.where(low, sums[0], sums[1]).astype(BF)
    out_ref[:, 128:192] = sums[2][:, :HD].astype(BF)


def call(kernel, outs, args, scratch=(), flops=10**9, moved=4 * 10**6, exps=0, vmem=LARGE):
    return pl.pallas_call(
        kernel,
        out_shape=[jax.ShapeDtypeStruct(shape, dtype) for shape, dtype in outs],
        scratch_shapes=list(scratch),
        in_specs=[
            pl.BlockSpec(memory_space=pltpu.SMEM if x.dtype == jnp.int32 else pltpu.VMEM) for x in args
        ],
        compiler_params=pltpu.CompilerParams(vmem_limit_bytes=vmem),
        cost_estimate=pl.CostEstimate(flops=flops, bytes_accessed=moved, transcendentals=exps),
    )(*args)


def to_markers(x):
    lead = x.shape[:-2]
    k = len(lead) + 1
    n = lax.axis_size("marker")
    me = lax.axis_index("marker")
    x = x.reshape(*lead, 6, n, 8, 512)
    out = x
    for step in (4, 3, 5, 2, 6, 1, 7):
        give = lax.dynamic_slice_in_dim(x, lax.rem(me + step, n), 1, k)
        got = lax.ppermute(give, "marker", [(i, (i + step) % n) for i in range(n)])
        out = lax.dynamic_update_slice_in_dim(out, got, lax.rem(me + n - step, n), k)
    return out.reshape(*lead, 384, 512)


def swapped(x, bit):
    n = lax.axis_size("batch")
    return lax.ppermute(x, "batch", [(i, i ^ bit) for i in range(n)])


def halves(x, shift):
    width = x.shape[1] // 2
    mine = (lax.axis_index("batch") >> shift) & 1
    keep = lax.dynamic_slice_in_dim(x, mine * width, width, 1)
    give = lax.dynamic_slice_in_dim(x, (1 - mine) * width, width, 1)
    return keep, give


def halve(x, bit, shift):
    keep, give = halves(x, shift)
    return (keep.astype(F32) + swapped(give, bit).astype(F32)).astype(BF)


def on_device(
    tokens, gain_first, w_qkv_space, w_out_space, gain_second, w_qkv_marker, w_out_marker, upstream
):
    both = ("space", "marker")
    rows = ("marker", "space")
    mine = jnp.transpose(tokens[0], (1, 0, 2)).reshape(384, 512)
    up_mine = jnp.transpose(upstream[0], (1, 0, 2)).reshape(384, 512)
    gain_1 = gain_first.reshape(1, 512)
    gain_2 = gain_second.reshape(1, 512)

    first_t, qkv_send = call(
        project_kernel,
        [((512, 384), BF), ((8, 64, 1152), BF)],
        (mine, gain_1, w_qkv_space),
    )
    qkv_one = lax.all_to_all(qkv_send, "space", 0, 0, tiled=True).reshape(512, 1152)
    wide = to_markers(jnp.stack([mine, up_mine]))
    first_all = lax.all_gather(first_t, "space", axis=0, tiled=False)

    heads, inv = call(
        spatial_kernel, [((512, 384), BF), ((6, 512), F32)], (qkv_one,),
        flops=2 * 10**9, exps=6 * 512 * 512, vmem=SMALL,
    )
    got = lax.all_to_all(heads, both, 0, 0, tiled=True).reshape(8, 64, 384)

    up_all = wide[1]
    core = (lax.axis_index("batch") & 1).astype(jnp.int32).reshape(1)
    keep, give, d_middle, d_send = call(
        middle_kernel,
        [((512, 1280), BF), ((512, 1280), BF), ((384, 512), BF), ((8, 64, 384), BF)],
        (core, got, wide[0], up_all, w_out_space, gain_2, w_qkv_marker, w_out_marker),
        scratch=[
            pltpu.VMEM(shape, BF)
            for shape in ((512, 2560), (384, 512), (384, 512), (384, 1536), (384, 512), (384, 1536), (384, 512))
        ],
        flops=6 * 10**9, exps=8 * 384 * 384, vmem=LARGE,
    )
    d_heads = lax.all_to_all(d_send.reshape(512, 384), both, 0, 0, tiled=True)

    d_heads, first_all = lax.optimization_barrier((d_heads, first_all))
    d_qkv_one, = call(
        spatial_back_kernel, [((512, 1152), BF)], (qkv_one, heads, inv, d_heads),
        flops=10**6, moved=10**4, vmem=SMALL,
    )
    middle_all = lax.all_gather(d_middle, "marker", axis=0, tiled=False)
    share, give = halves((keep.astype(F32) + swapped(give, 1).astype(F32)).astype(BF), 1)
    give = swapped(give, 2)
    d_qkv_one, give = lax.optimization_barrier((d_qkv_one, give))
    d_back = lax.all_to_all(d_qkv_one, "space", 0, 0, tiled=True).reshape(8, 64, 1152)
    first_all, middle_all = lax.optimization_barrier((first_all, middle_all))
    share = (share.astype(F32) + give.astype(F32)).astype(BF)
    column, = call(column_kernel, [((512, 192), BF)], (first_all, d_qkv_one), flops=2 * 10**9)
    shares = jnp.concatenate([share, column], axis=1)
    shares, d_back = lax.optimization_barrier((shares, d_back))
    d_middle_mine = lax.dynamic_index_in_dim(
        middle_all.reshape(8, 6, 8, 8, 512), lax.axis_index("marker"), 2, keepdims=False
    )
    d_middle_mine = jnp.transpose(d_middle_mine, (1, 0, 2, 3)).reshape(384, 512)
    shares = lax.all_to_all(shares, rows, 0, 0, tiled=True).reshape(8, 8, 8, 832).astype(F32)
    column = jnp.sum(shares[..., 640:], axis=0).transpose(1, 0, 2).reshape(8, 1536)
    share = jnp.sum(shares[..., :640], axis=(0, 1))
    share = jnp.concatenate([share, column], axis=1).astype(BF)
    share = lax.all_gather(share, "batch", axis=0, tiled=False)
    share = share.reshape(2, 2, 8, 2176).astype(F32)
    column = jnp.sum(share[..., 640:], axis=(0, 1))
    share = share[..., :640].transpose(2, 1, 0, 3).reshape(8, 2560)
    d_tokens, = call(
        last_kernel, [((384, 512), BF)], (d_back, w_qkv_space, mine, gain_1, d_middle_mine),
        scratch=[pltpu.VMEM((384, 1536), BF)], vmem=SMALL,
    )

    count = 1
    for axis in ("batch", "marker", "space"):
        count *= lax.axis_size(axis)
    factor = 1.0 / math.sqrt(count * 384)
    at = (lax.axis_index("marker") * 8 + lax.axis_index("space")) * 8

    own = [lax.dynamic_slice_in_dim(x, at, 8, 0) for x in (w_qkv_space, gain_first, w_qkv_marker, gain_second)]
    own = lax.optimization_barrier(own)

    def gain_grad(weight, gain, grad):
        return jnp.sum(weight.astype(F32) * grad, axis=1) / gain

    g_qkv_space = column * factor
    g_qkv_marker = share[:, :1536] * factor
    return (
        jnp.transpose(d_tokens.reshape(6, 64, 512), (1, 0, 2))[None],
        g_qkv_space,
        share[:, 1536:2048] * factor,
        gain_grad(own[0], own[1], g_qkv_space),
        g_qkv_marker,
        share[:, 2048:] * factor,
        gain_grad(own[2], own[3], g_qkv_marker),
    )


def solution(mesh):
    in_specs = (
        P("batch", "space", "marker", None),
        P(), P(), P(), P(), P(), P(),
        P("batch", "space", "marker", None),
    )
    shares = P(("marker", "space"), None)
    out_specs = (
        P("batch", "space", "marker", None),
        shares,
        shares,
        P(("marker", "space")),
        shares,
        shares,
        P(("marker", "space")),
    )
    return jax.shard_map(
        on_device, mesh=mesh, in_specs=in_specs, out_specs=out_specs, check_vma=False
    )
```

```python
import functools
import math

import jax
import jax.numpy as jnp
from jax import lax
from jax.experimental import pallas as pl
from jax.experimental.pallas import tpu as pltpu
from jax.sharding import PartitionSpec as P

HD = 64
EPS = 1e-06
BF = jnp.bfloat16
F32 = jnp.float32
LOG2E = math.log2(math.e)
SMALL = 24 * 1024 * 1024
LARGE = 56 * 1024 * 1024


def low_half(rows, width=128):
    return lax.broadcasted_iota(jnp.int32, (rows, width), 1) % 128 < HD


def swap(x):
    return pltpu.roll(x, HD, 1)


def dot(a, b):
    return jnp.dot(a, b, preferred_element_type=F32)


def dot_nt(a, b):
    return lax.dot_general(a, b, (((1,), (1,)), ((), ())), preferred_element_type=F32)


def outer(left, right):
    return lax.dot_general(
        left, right, (((0,), (0,)), ((), ())), preferred_element_type=F32
    ).astype(BF)


def half_mean(x, lo):
    first = jnp.sum(jnp.where(lo, x, 0.0), axis=-1, keepdims=True)
    second = jnp.sum(jnp.where(lo, 0.0, x), axis=-1, keepdims=True)
    return jnp.where(lo, first, second) * (1.0 / HD)


def half_scale(x, lo):
    return lax.rsqrt(half_mean(x * x, lo) + EPS)


def only_half(x, unit):
    own = x[unit * HD : (unit + 1) * HD]
    zero = jnp.zeros_like(own)
    return jnp.concatenate([own, zero] if unit == 0 else [zero, own], axis=0)


def row_scale(x):
    return lax.rsqrt(jnp.mean(x * x, axis=-1, keepdims=True) + EPS)


def norm_back(x, gain, cotangent):
    scale = row_scale(x)
    unit = x * scale
    pulled = cotangent * gain
    return scale * (pulled - unit * jnp.mean(pulled * unit, axis=-1, keepdims=True))


def scaled_pair(query, keys, lo):
    q_scale = half_scale(query, lo)
    k_scale = half_scale(keys, lo)
    return query * q_scale, q_scale, keys * k_scale, k_scale


def pair_back(d_qn, d_kn, qn, q_scale, kn, k_scale, lo):
    d_q = q_scale * (d_qn - qn * half_mean(d_qn * qn, lo))
    d_k = k_scale * (d_kn - kn * half_mean(d_kn * kn, lo))
    return d_q, d_k


def project_kernel(tokens_ref, gain_ref, w_ref, first_t_ref, send_ref):
    lo = low_half(64)
    x = tokens_ref[...].astype(F32)
    first = (x * row_scale(x) * gain_ref[...]).astype(BF)
    first_t_ref[...] = first.astype(F32).T.astype(BF)
    for hh in range(4):
        wide = dot(first, w_ref[:, hh * 384 : (hh + 1) * 384])
        for jj in range(3):
            a = wide[(2 * jj) * 64 : (2 * jj + 1) * 64]
            b = wide[(2 * jj + 1) * 64 : (2 * jj + 2) * 64]
            for block in range(3):
                ba = a[:, block * 128 : (block + 1) * 128]
                bb = b[:, block * 128 : (block + 1) * 128]
                left = jnp.where(lo, ba, swap(bb)).astype(BF)
                right = jnp.where(lo, swap(ba), bb).astype(BF)
                for half, value in ((0, left), (1, right)):
                    part = 2 * block + half
                    head, kind = 2 * hh + part // 3, part % 3
                    at = jj * 384 + kind * 128
                    send_ref[head, :, at : at + 128] = value


def spatial_kernel(qkv_ref, heads_ref, inv_ref):
    length = qkv_ref.shape[0]
    lo = low_half(length)
    step = 256
    for jj in range(3):
        at = jj * 384
        query = qkv_ref[:, at : at + 128].astype(F32)
        keys = qkv_ref[:, at + 128 : at + 256].astype(F32)
        values = qkv_ref[:, at + 256 : at + 384].astype(F32)
        qn, _, kn, _ = scaled_pair(query, keys, lo)
        q_t = (qn * (LOG2E / 8.0)).T.astype(BF)
        kb = kn.astype(BF)
        v_t = values.T.astype(BF)
        out = []
        for unit in range(2):
            q_own = only_half(q_t, unit)
            cols = []
            for start in range(0, length, step):
                e = jnp.exp2(dot(kb, q_own[:, start : start + step]))
                inv = 1.0 / jnp.sum(e, axis=0, keepdims=True)
                inv_ref[2 * jj + unit : 2 * jj + unit + 1, start : start + step] = inv
                cols.append(dot(v_t[unit * HD : (unit + 1) * HD], e.astype(BF)) * inv)
            out.append(jnp.concatenate(cols, axis=1))
        heads_ref[:, jj * 128 : (jj + 1) * 128] = jnp.concatenate(out, axis=0).T.astype(BF)


def spatial_back_kernel(qkv_ref, heads_ref, inv_ref, d_heads_ref, d_qkv_ref):
    length = qkv_ref.shape[0]
    lo = low_half(length)
    step = 256
    for jj in range(3):
        at = jj * 384
        query = qkv_ref[:, at : at + 128].astype(F32)
        keys = qkv_ref[:, at + 128 : at + 256].astype(F32)
        vb = qkv_ref[:, at + 256 : at + 384]
        qn, q_scale, kn, k_scale = scaled_pair(query, keys, lo)
        qs = qn * (LOG2E / 8.0)
        q_t = qs.T.astype(BF)
        qb = qs.astype(BF)
        kb = kn.astype(BF)
        k_t = kn.T.astype(BF)
        o_t = heads_ref[:, jj * 128 : (jj + 1) * 128].astype(F32).T
        g_t = d_heads_ref[:, jj * 128 : (jj + 1) * 128].astype(F32).T
        scaled, drops = [], []
        for unit in range(2):
            rows = slice(unit * HD, (unit + 1) * HD)
            own = g_t[rows] * inv_ref[2 * jj + unit : 2 * jj + unit + 1, :]
            scaled.append(own)
            drops.append(jnp.sum(own * o_t[rows], axis=0, keepdims=True))
        g_scaled = jnp.concatenate(scaled, axis=0)
        gb = g_scaled.T.astype(BF)
        g_scaled = g_scaled.astype(BF)
        d_q, d_k, d_v = [], [], []
        for unit in range(2):
            q_own = only_half(q_t, unit)
            g_own = only_half(g_scaled, unit)
            cols, dk, dv = [], 0.0, 0.0
            for start in range(0, length, step):
                part = slice(start, start + step)
                e = jnp.exp2(dot(kb, q_own[:, part]))
                ds = (e * (dot(vb, g_own[:, part]) - drops[unit][:, part])).astype(BF)
                cols.append(dot(k_t[unit * HD : (unit + 1) * HD], ds))
                dk = dk + dot(ds, qb[part])
                dv = dv + dot(e.astype(BF), gb[part])
            d_q.append(jnp.concatenate(cols, axis=1))
            d_k.append(dk)
            d_v.append(dv)
        d_qn = jnp.concatenate(d_q, axis=0).T * (1.0 / 8.0)
        d_kn = jnp.where(lo, d_k[0], d_k[1]) * (1.0 / LOG2E)
        dq, dk = pair_back(d_qn, d_kn, qn, q_scale, kn, k_scale, lo)
        d_qkv_ref[:, at : at + 128] = dq.astype(BF)
        d_qkv_ref[:, at + 128 : at + 256] = dk.astype(BF)
        d_qkv_ref[:, at + 256 : at + 384] = jnp.where(lo, d_v[0], d_v[1]).astype(BF)


def middle_kernel(
    core_ref, got_ref, tokens_ref, up_ref, w_out_ref, gain_ref, w_qkv_ref, w_last_ref,
    keep_ref, give_ref, d_middle_ref, send_ref,
    grads_ref, heads_one_ref, second_ref, d_qkv_ref, heads_two_ref, qkv_ref, d_two_ref,
):
    lo64 = low_half(64)
    for hh in range(4):
        for jj in range(3):
            a = got_ref[2 * hh, :, jj * 128 : (jj + 1) * 128].astype(F32)
            b = got_ref[2 * hh + 1, :, jj * 128 : (jj + 1) * 128].astype(F32)
            cols = slice(hh * 128, (hh + 1) * 128)
            heads_one_ref[(2 * jj) * 64 : (2 * jj + 1) * 64, cols] = jnp.where(lo64, a, swap(b)).astype(BF)
            heads_one_ref[(2 * jj + 1) * 64 : (2 * jj + 2) * 64, cols] = jnp.where(lo64, swap(a), b).astype(BF)
    middle = tokens_ref[...].astype(F32) + dot(heads_one_ref[...], w_out_ref[...])
    middle = middle.astype(BF).astype(F32)
    gain = gain_ref[...]
    second = (middle * row_scale(middle) * gain).astype(BF)
    second_ref[...] = second
    qkv_ref[...] = dot(second, w_qkv_ref[...]).astype(BF)
    d_two_ref[...] = dot_nt(up_ref[...], w_last_ref[...]).astype(BF)

    length = qkv_ref.shape[0]
    lo = low_half(length)
    same = (
        lax.broadcasted_iota(jnp.int32, (length, length), 0) % 8
        == lax.broadcasted_iota(jnp.int32, (length, length), 1) % 8
    )
    for hh in range(4):
        at = hh * 384
        b0 = qkv_ref[:, at : at + 128].astype(F32)
        b1 = qkv_ref[:, at + 128 : at + 256].astype(F32)
        b2 = qkv_ref[:, at + 256 : at + 384].astype(F32)
        query = jnp.where(lo, b0, b1)
        keys = swap(jnp.where(lo, b2, b0))
        values = jnp.where(lo, b1, b2)
        qn, q_scale, kn, k_scale = scaled_pair(query, keys, lo)
        qs = qn * (LOG2E / 8.0)
        q_t = qs.T.astype(BF)
        qb = qs.astype(BF)
        kb = kn.astype(BF)
        k_t = kn.T.astype(BF)
        vb = values.astype(BF)
        v_t = values.T.astype(BF)
        g_t = d_two_ref[:, hh * 128 : (hh + 1) * 128].astype(F32).T
        o_t, d_q, d_k, d_v = [], [], [], []
        for unit in range(2):
            rows = slice(unit * HD, (unit + 1) * HD)
            e = jnp.where(same, jnp.exp2(dot(kb, only_half(q_t, unit))), 0.0)
            inv = 1.0 / jnp.sum(e, axis=0, keepdims=True)
            eb = e.astype(BF)
            o = dot(v_t[rows], eb) * inv
            own = g_t[rows] * inv
            drop = jnp.sum(own * o, axis=0, keepdims=True)
            zero = jnp.zeros_like(own)
            g_own = jnp.concatenate([own, zero] if unit == 0 else [zero, own], axis=0)
            gb = g_own.T.astype(BF)
            ds = (e * (dot(vb, g_own.astype(BF)) - drop)).astype(BF)
            o_t.append(o)
            d_q.append(dot(k_t[rows], ds))
            d_k.append(dot(ds, qb))
            d_v.append(dot(eb, gb))
        heads_two_ref[:, hh * 128 : (hh + 1) * 128] = jnp.concatenate(o_t, axis=0).T.astype(BF)
        d_qn = jnp.concatenate(d_q, axis=0).T * (1.0 / 8.0)
        d_kn = jnp.where(lo, d_k[0], d_k[1]) * (1.0 / LOG2E)
        dq, dk = pair_back(d_qn, d_kn, qn, q_scale, kn, k_scale, lo)
        dv = jnp.where(lo, d_v[0], d_v[1])
        dk = swap(dk)
        d_qkv_ref[:, at : at + 128] = jnp.where(lo, dq, dk).astype(BF)
        d_qkv_ref[:, at + 128 : at + 256] = jnp.where(lo, dv, dq).astype(BF)
        d_qkv_ref[:, at + 256 : at + 384] = jnp.where(lo, dk, dv).astype(BF)

    d_second = dot_nt(d_qkv_ref[...], w_qkv_ref[...]).astype(BF).astype(F32)
    d_middle = (up_ref[...].astype(F32) + norm_back(middle, gain, d_second)).astype(BF)
    d_middle_ref[...] = d_middle
    d_heads = dot_nt(d_middle, w_out_ref[...])
    for hh in range(4):
        for jj in range(3):
            a = d_heads[(2 * jj) * 64 : (2 * jj + 1) * 64, hh * 128 : (hh + 1) * 128]
            b = d_heads[(2 * jj + 1) * 64 : (2 * jj + 2) * 64, hh * 128 : (hh + 1) * 128]
            cols = slice(jj * 128, (jj + 1) * 128)
            send_ref[2 * hh, :, cols] = jnp.where(lo64, a, swap(b)).astype(BF)
            send_ref[2 * hh + 1, :, cols] = jnp.where(lo64, swap(a), b).astype(BF)
    grads_ref[:, :1536] = outer(second_ref[...], d_qkv_ref[...])
    grads_ref[:, 1536:2048] = outer(heads_one_ref[...], d_middle)
    grads_ref[:, 2048:] = outer(heads_two_ref[...], up_ref[...])
    core = core_ref[0]
    keep_ref[...] = grads_ref[:, pl.ds(pl.multiple_of(core * 1280, 1280), 1280)]
    give_ref[...] = grads_ref[:, pl.ds(pl.multiple_of((1 - core) * 1280, 1280), 1280)]


def last_kernel(got_ref, w_ref, tokens_ref, gain_ref, d_middle_ref, out_ref, d_qkv_ref):
    lo = low_half(64)
    for hh in range(4):
        for jj in range(3):
            part = []
            for head in (2 * hh, 2 * hh + 1):
                for kind in range(3):
                    at = jj * 384 + kind * 128
                    part.append(got_ref[head, :, at : at + 128].astype(F32))
            for block in range(3):
                left, right = part[2 * block], part[2 * block + 1]
                at = hh * 384 + block * 128
                d_qkv_ref[(2 * jj) * 64 : (2 * jj + 1) * 64, at : at + 128] = jnp.where(
                    lo, left, swap(right)
                ).astype(BF)
                d_qkv_ref[(2 * jj + 1) * 64 : (2 * jj + 2) * 64, at : at + 128] = jnp.where(
                    lo, swap(left), right
                ).astype(BF)
    d_first = dot_nt(d_qkv_ref[...], w_ref[...]).astype(BF).astype(F32)
    x = tokens_ref[...].astype(F32)
    out_ref[...] = (
        d_middle_ref[...].astype(F32) + norm_back(x, gain_ref[...], d_first)
    ).astype(BF)


def column_kernel(first_ref, d_qkv_ref, out_ref):
    lo = low_half(64, 384)
    total = jnp.zeros((512, 384), F32)
    for s in range(8):
        rows = []
        for jj in range(3):
            block = d_qkv_ref[s * 64 : (s + 1) * 64, jj * 384 : (jj + 1) * 384].astype(F32)
            rows.append(jnp.where(lo, block, 0.0).astype(BF))
            rows.append(jnp.where(lo, 0.0, block).astype(BF))
        total = total + dot(first_ref[s], jnp.concatenate(rows, axis=0))
    low = low_half(512)
    sums = [total[:, i * 128 : (i + 1) * 128] for i in range(3)]
    sums = [x + swap(x) for x in sums]
    out_ref[:, 0:128] = jnp.where(low, sums[0], sums[1]).astype(BF)
    out_ref[:, 128:192] = sums[2][:, :HD].astype(BF)


def call(kernel, outs, args, scratch=(), flops=10**9, moved=4 * 10**6, exps=0, vmem=LARGE):
    return pl.pallas_call(
        kernel,
        out_shape=[jax.ShapeDtypeStruct(shape, dtype) for shape, dtype in outs],
        scratch_shapes=list(scratch),
        in_specs=[
            pl.BlockSpec(memory_space=pltpu.SMEM if x.dtype == jnp.int32 else pltpu.VMEM) for x in args
        ],
        compiler_params=pltpu.CompilerParams(vmem_limit_bytes=vmem),
        cost_estimate=pl.CostEstimate(flops=flops, bytes_accessed=moved, transcendentals=exps),
    )(*args)


def to_markers(x):
    lead = x.shape[:-2]
    k = len(lead) + 1
    n = lax.axis_size("marker")
    me = lax.axis_index("marker")
    x = x.reshape(*lead, 6, n, 8, 512)
    out = x
    for step in (4, 3, 5, 2, 6, 1, 7):
        give = lax.dynamic_slice_in_dim(x, lax.rem(me + step, n), 1, k)
        got = lax.ppermute(give, "marker", [(i, (i + step) % n) for i in range(n)])
        out = lax.dynamic_update_slice_in_dim(out, got, lax.rem(me + n - step, n), k)
    return out.reshape(*lead, 384, 512)


def swapped(x, bit):
    n = lax.axis_size("batch")
    return lax.ppermute(x, "batch", [(i, i ^ bit) for i in range(n)])


def halves(x, shift):
    width = x.shape[1] // 2
    mine = (lax.axis_index("batch") >> shift) & 1
    keep = lax.dynamic_slice_in_dim(x, mine * width, width, 1)
    give = lax.dynamic_slice_in_dim(x, (1 - mine) * width, width, 1)
    return keep, give


def halve(x, bit, shift):
    keep, give = halves(x, shift)
    return (keep.astype(F32) + swapped(give, bit).astype(F32)).astype(BF)


def on_device(
    tokens, gain_first, w_qkv_space, w_out_space, gain_second, w_qkv_marker, w_out_marker, upstream
):
    both = ("space", "marker")
    rows = ("marker", "space")
    mine = jnp.transpose(tokens[0], (1, 0, 2)).reshape(384, 512)
    up_mine = jnp.transpose(upstream[0], (1, 0, 2)).reshape(384, 512)
    gain_1 = gain_first.reshape(1, 512)
    gain_2 = gain_second.reshape(1, 512)

    first_t, qkv_send = call(
        project_kernel,
        [((512, 384), BF), ((8, 64, 1152), BF)],
        (mine, gain_1, w_qkv_space),
    )
    qkv_one = lax.all_to_all(qkv_send, "space", 0, 0, tiled=True).reshape(512, 1152)
    wide = to_markers(jnp.stack([mine, up_mine]))
    first_all = lax.all_gather(first_t, "space", axis=0, tiled=False)

    heads, inv = call(
        spatial_kernel, [((512, 384), BF), ((6, 512), F32)], (qkv_one,),
        flops=2 * 10**9, exps=6 * 512 * 512, vmem=SMALL,
    )
    got = lax.all_to_all(heads, both, 0, 0, tiled=True).reshape(8, 64, 384)

    up_all = wide[1]
    core = (lax.axis_index("batch") & 1).astype(jnp.int32).reshape(1)
    keep, give, d_middle, d_send = call(
        middle_kernel,
        [((512, 1280), BF), ((512, 1280), BF), ((384, 512), BF), ((8, 64, 384), BF)],
        (core, got, wide[0], up_all, w_out_space, gain_2, w_qkv_marker, w_out_marker),
        scratch=[
            pltpu.VMEM(shape, BF)
            for shape in ((512, 2560), (384, 512), (384, 512), (384, 1536), (384, 512), (384, 1536), (384, 512))
        ],
        flops=6 * 10**9, exps=8 * 384 * 384, vmem=LARGE,
    )
    d_heads = lax.all_to_all(d_send.reshape(512, 384), both, 0, 0, tiled=True)

    d_heads, first_all = lax.optimization_barrier((d_heads, first_all))
    d_qkv_one, = call(
        spatial_back_kernel, [((512, 1152), BF)], (qkv_one, heads, inv, d_heads),
        flops=10**6, moved=10**4, vmem=SMALL,
    )
    middle_all = lax.all_gather(d_middle, "marker", axis=0, tiled=False)
    share, give = halves((keep.astype(F32) + swapped(give, 1).astype(F32)).astype(BF), 1)
    give = swapped(give, 2)
    d_qkv_one, give = lax.optimization_barrier((d_qkv_one, give))
    d_back = lax.all_to_all(d_qkv_one, "space", 0, 0, tiled=True).reshape(8, 64, 1152)
    give, middle_all = lax.optimization_barrier((give, middle_all))
    share = (share.astype(F32) + give.astype(F32)).astype(BF)
    column, = call(column_kernel, [((512, 192), BF)], (first_all, d_qkv_one), flops=2 * 10**9)
    shares = jnp.concatenate([share, halve(column, 1, 0)], axis=1)
    shares, d_back = lax.optimization_barrier((shares, d_back))
    d_middle_mine = lax.dynamic_index_in_dim(
        middle_all.reshape(8, 6, 8, 8, 512), lax.axis_index("marker"), 2, keepdims=False
    )
    d_middle_mine = jnp.transpose(d_middle_mine, (1, 0, 2, 3)).reshape(384, 512)
    shares = lax.all_to_all(shares, rows, 0, 0, tiled=True).reshape(8, 8, 8, 736).astype(F32)
    column = jnp.sum(shares[..., 640:], axis=0).transpose(1, 0, 2).reshape(8, 768)
    share = jnp.sum(shares[..., :640], axis=(0, 1))
    share = jnp.concatenate([share, column], axis=1).astype(BF)
    share = lax.all_gather(share, "batch", axis=0, tiled=False)
    share = share.reshape(2, 2, 8, 1408).astype(F32)
    column = jnp.sum(share[..., 640:], axis=0).reshape(2, 8, 8, 96)
    column = column.transpose(1, 2, 0, 3).reshape(8, 1536)
    share = share[..., :640].transpose(2, 1, 0, 3).reshape(8, 2560)
    d_tokens, = call(
        last_kernel, [((384, 512), BF)], (d_back, w_qkv_space, mine, gain_1, d_middle_mine),
        scratch=[pltpu.VMEM((384, 1536), BF)], vmem=SMALL,
    )

    count = 1
    for axis in ("batch", "marker", "space"):
        count *= lax.axis_size(axis)
    factor = 1.0 / math.sqrt(count * 384)
    at = (lax.axis_index("marker") * 8 + lax.axis_index("space")) * 8

    own = [lax.dynamic_slice_in_dim(x, at, 8, 0) for x in (w_qkv_space, gain_first, w_qkv_marker, gain_second)]
    own = lax.optimization_barrier(own)

    def gain_grad(weight, gain, grad):
        return jnp.sum(weight.astype(F32) * grad, axis=1) / gain

    g_qkv_space = column * factor
    g_qkv_marker = share[:, :1536] * factor
    return (
        jnp.transpose(d_tokens.reshape(6, 64, 512), (1, 0, 2))[None],
        g_qkv_space,
        share[:, 1536:2048] * factor,
        gain_grad(own[0], own[1], g_qkv_space),
        g_qkv_marker,
        share[:, 2048:] * factor,
        gain_grad(own[2], own[3], g_qkv_marker),
    )


def solution(mesh):
    in_specs = (
        P("batch", "space", "marker", None),
        P(), P(), P(), P(), P(), P(),
        P("batch", "space", "marker", None),
    )
    shares = P(("marker", "space"), None)
    out_specs = (
        P("batch", "space", "marker", None),
        shares,
        shares,
        P(("marker", "space")),
        shares,
        shares,
        P(("marker", "space")),
    )
    return jax.shard_map(
        on_device, mesh=mesh, in_specs=in_specs, out_specs=out_specs, check_vma=False
    )
```

```python
import functools
import math

import jax
import jax.numpy as jnp
from jax import lax
from jax.experimental import pallas as pl
from jax.experimental.pallas import tpu as pltpu
from jax.sharding import PartitionSpec as P

HD = 64
EPS = 1e-06
BF = jnp.bfloat16
F32 = jnp.float32
LOG2E = math.log2(math.e)
SMALL = 24 * 1024 * 1024
LARGE = 56 * 1024 * 1024


def low_half(rows, width=128):
    return lax.broadcasted_iota(jnp.int32, (rows, width), 1) % 128 < HD


def swap(x):
    return pltpu.roll(x, HD, 1)


def dot(a, b):
    return jnp.dot(a, b, preferred_element_type=F32)


def dot_nt(a, b):
    return lax.dot_general(a, b, (((1,), (1,)), ((), ())), preferred_element_type=F32)


def outer(left, right):
    return lax.dot_general(
        left, right, (((0,), (0,)), ((), ())), preferred_element_type=F32
    ).astype(BF)


def half_mean(x, lo):
    first = jnp.sum(jnp.where(lo, x, 0.0), axis=-1, keepdims=True)
    second = jnp.sum(jnp.where(lo, 0.0, x), axis=-1, keepdims=True)
    return jnp.where(lo, first, second) * (1.0 / HD)


def half_scale(x, lo):
    return lax.rsqrt(half_mean(x * x, lo) + EPS)


def only_half(x, unit):
    own = x[unit * HD : (unit + 1) * HD]
    zero = jnp.zeros_like(own)
    return jnp.concatenate([own, zero] if unit == 0 else [zero, own], axis=0)


def row_scale(x):
    return lax.rsqrt(jnp.mean(x * x, axis=-1, keepdims=True) + EPS)


def norm_back(x, gain, cotangent):
    scale = row_scale(x)
    unit = x * scale
    pulled = cotangent * gain
    return scale * (pulled - unit * jnp.mean(pulled * unit, axis=-1, keepdims=True))


def scaled_pair(query, keys, lo):
    q_scale = half_scale(query, lo)
    k_scale = half_scale(keys, lo)
    return query * q_scale, q_scale, keys * k_scale, k_scale


def pair_back(d_qn, d_kn, qn, q_scale, kn, k_scale, lo):
    d_q = q_scale * (d_qn - qn * half_mean(d_qn * qn, lo))
    d_k = k_scale * (d_kn - kn * half_mean(d_kn * kn, lo))
    return d_q, d_k


def project_kernel(tokens_ref, gain_ref, w_ref, first_t_ref, send_ref):
    lo = low_half(64)
    x = tokens_ref[...].astype(F32)
    first = (x * row_scale(x) * gain_ref[...]).astype(BF)
    first_t_ref[...] = first.astype(F32).T.astype(BF)
    for hh in range(4):
        wide = dot(first, w_ref[:, hh * 384 : (hh + 1) * 384])
        for jj in range(3):
            a = wide[(2 * jj) * 64 : (2 * jj + 1) * 64]
            b = wide[(2 * jj + 1) * 64 : (2 * jj + 2) * 64]
            for block in range(3):
                ba = a[:, block * 128 : (block + 1) * 128]
                bb = b[:, block * 128 : (block + 1) * 128]
                left = jnp.where(lo, ba, swap(bb)).astype(BF)
                right = jnp.where(lo, swap(ba), bb).astype(BF)
                for half, value in ((0, left), (1, right)):
                    part = 2 * block + half
                    head, kind = 2 * hh + part // 3, part % 3
                    at = jj * 384 + kind * 128
                    send_ref[head, :, at : at + 128] = value


def spatial_kernel(qkv_ref, heads_ref, inv_ref):
    length = qkv_ref.shape[0]
    lo = low_half(length)
    step = 512
    for jj in range(3):
        at = jj * 384
        query = qkv_ref[:, at : at + 128].astype(F32)
        keys = qkv_ref[:, at + 128 : at + 256].astype(F32)
        values = qkv_ref[:, at + 256 : at + 384].astype(F32)
        qn, _, kn, _ = scaled_pair(query, keys, lo)
        q_t = (qn * (LOG2E / 8.0)).T.astype(BF)
        kb = kn.astype(BF)
        v_t = values.T.astype(BF)
        out = []
        for unit in range(2):
            q_own = only_half(q_t, unit)
            cols = []
            for start in range(0, length, step):
                e = jnp.exp2(dot(kb, q_own[:, start : start + step]))
                inv = 1.0 / jnp.sum(e, axis=0, keepdims=True)
                inv_ref[2 * jj + unit : 2 * jj + unit + 1, start : start + step] = inv
                cols.append(dot(v_t[unit * HD : (unit + 1) * HD], e.astype(BF)) * inv)
            out.append(jnp.concatenate(cols, axis=1))
        heads_ref[:, jj * 128 : (jj + 1) * 128] = jnp.concatenate(out, axis=0).T.astype(BF)


def spatial_back_kernel(qkv_ref, heads_ref, inv_ref, d_heads_ref, d_qkv_ref):
    length = qkv_ref.shape[0]
    lo = low_half(length)
    step = 512
    for jj in range(3):
        at = jj * 384
        query = qkv_ref[:, at : at + 128].astype(F32)
        keys = qkv_ref[:, at + 128 : at + 256].astype(F32)
        vb = qkv_ref[:, at + 256 : at + 384]
        qn, q_scale, kn, k_scale = scaled_pair(query, keys, lo)
        qs = qn * (LOG2E / 8.0)
        q_t = qs.T.astype(BF)
        qb = qs.astype(BF)
        kb = kn.astype(BF)
        k_t = kn.T.astype(BF)
        o_t = heads_ref[:, jj * 128 : (jj + 1) * 128].astype(F32).T
        g_t = d_heads_ref[:, jj * 128 : (jj + 1) * 128].astype(F32).T
        scaled, drops = [], []
        for unit in range(2):
            rows = slice(unit * HD, (unit + 1) * HD)
            own = g_t[rows] * inv_ref[2 * jj + unit : 2 * jj + unit + 1, :]
            scaled.append(own)
            drops.append(jnp.sum(own * o_t[rows], axis=0, keepdims=True))
        g_scaled = jnp.concatenate(scaled, axis=0)
        gb = g_scaled.T.astype(BF)
        g_scaled = g_scaled.astype(BF)
        d_q, d_k, d_v = [], [], []
        for unit in range(2):
            q_own = only_half(q_t, unit)
            g_own = only_half(g_scaled, unit)
            cols, dk, dv = [], 0.0, 0.0
            for start in range(0, length, step):
                part = slice(start, start + step)
                e = jnp.exp2(dot(kb, q_own[:, part]))
                ds = (e * (dot(vb, g_own[:, part]) - drops[unit][:, part])).astype(BF)
                cols.append(dot(k_t[unit * HD : (unit + 1) * HD], ds))
                dk = dk + dot(ds, qb[part])
                dv = dv + dot(e.astype(BF), gb[part])
            d_q.append(jnp.concatenate(cols, axis=1))
            d_k.append(dk)
            d_v.append(dv)
        d_qn = jnp.concatenate(d_q, axis=0).T * (1.0 / 8.0)
        d_kn = jnp.where(lo, d_k[0], d_k[1]) * (1.0 / LOG2E)
        dq, dk = pair_back(d_qn, d_kn, qn, q_scale, kn, k_scale, lo)
        d_qkv_ref[:, at : at + 128] = dq.astype(BF)
        d_qkv_ref[:, at + 128 : at + 256] = dk.astype(BF)
        d_qkv_ref[:, at + 256 : at + 384] = jnp.where(lo, d_v[0], d_v[1]).astype(BF)


def middle_kernel(
    core_ref, got_ref, tokens_ref, up_ref, w_out_ref, gain_ref, w_qkv_ref, w_last_ref,
    keep_ref, give_ref, d_middle_ref, send_ref,
    grads_ref, heads_one_ref, second_ref, d_qkv_ref, heads_two_ref, qkv_ref, d_two_ref,
):
    lo64 = low_half(64)
    for hh in range(4):
        for jj in range(3):
            a = got_ref[2 * hh, :, jj * 128 : (jj + 1) * 128].astype(F32)
            b = got_ref[2 * hh + 1, :, jj * 128 : (jj + 1) * 128].astype(F32)
            cols = slice(hh * 128, (hh + 1) * 128)
            heads_one_ref[(2 * jj) * 64 : (2 * jj + 1) * 64, cols] = jnp.where(lo64, a, swap(b)).astype(BF)
            heads_one_ref[(2 * jj + 1) * 64 : (2 * jj + 2) * 64, cols] = jnp.where(lo64, swap(a), b).astype(BF)
    middle = tokens_ref[...].astype(F32) + dot(heads_one_ref[...], w_out_ref[...])
    middle = middle.astype(BF).astype(F32)
    gain = gain_ref[...]
    second = (middle * row_scale(middle) * gain).astype(BF)
    second_ref[...] = second
    qkv_ref[...] = dot(second, w_qkv_ref[...]).astype(BF)
    d_two_ref[...] = dot_nt(up_ref[...], w_last_ref[...]).astype(BF)

    length = qkv_ref.shape[0]
    lo = low_half(length)
    same = (
        lax.broadcasted_iota(jnp.int32, (length, length), 0) % 8
        == lax.broadcasted_iota(jnp.int32, (length, length), 1) % 8
    )
    for hh in range(4):
        at = hh * 384
        b0 = qkv_ref[:, at : at + 128].astype(F32)
        b1 = qkv_ref[:, at + 128 : at + 256].astype(F32)
        b2 = qkv_ref[:, at + 256 : at + 384].astype(F32)
        query = jnp.where(lo, b0, b1)
        keys = swap(jnp.where(lo, b2, b0))
        values = jnp.where(lo, b1, b2)
        qn, q_scale, kn, k_scale = scaled_pair(query, keys, lo)
        qs = qn * (LOG2E / 8.0)
        q_t = qs.T.astype(BF)
        qb = qs.astype(BF)
        kb = kn.astype(BF)
        k_t = kn.T.astype(BF)
        vb = values.astype(BF)
        v_t = values.T.astype(BF)
        g_t = d_two_ref[:, hh * 128 : (hh + 1) * 128].astype(F32).T
        o_t, d_q, d_k, d_v = [], [], [], []
        for unit in range(2):
            rows = slice(unit * HD, (unit + 1) * HD)
            e = jnp.where(same, jnp.exp2(dot(kb, only_half(q_t, unit))), 0.0)
            inv = 1.0 / jnp.sum(e, axis=0, keepdims=True)
            eb = e.astype(BF)
            o = dot(v_t[rows], eb) * inv
            own = g_t[rows] * inv
            drop = jnp.sum(own * o, axis=0, keepdims=True)
            zero = jnp.zeros_like(own)
            g_own = jnp.concatenate([own, zero] if unit == 0 else [zero, own], axis=0)
            gb = g_own.T.astype(BF)
            ds = (e * (dot(vb, g_own.astype(BF)) - drop)).astype(BF)
            o_t.append(o)
            d_q.append(dot(k_t[rows], ds))
            d_k.append(dot(ds, qb))
            d_v.append(dot(eb, gb))
        heads_two_ref[:, hh * 128 : (hh + 1) * 128] = jnp.concatenate(o_t, axis=0).T.astype(BF)
        d_qn = jnp.concatenate(d_q, axis=0).T * (1.0 / 8.0)
        d_kn = jnp.where(lo, d_k[0], d_k[1]) * (1.0 / LOG2E)
        dq, dk = pair_back(d_qn, d_kn, qn, q_scale, kn, k_scale, lo)
        dv = jnp.where(lo, d_v[0], d_v[1])
        dk = swap(dk)
        d_qkv_ref[:, at : at + 128] = jnp.where(lo, dq, dk).astype(BF)
        d_qkv_ref[:, at + 128 : at + 256] = jnp.where(lo, dv, dq).astype(BF)
        d_qkv_ref[:, at + 256 : at + 384] = jnp.where(lo, dk, dv).astype(BF)

    d_second = dot_nt(d_qkv_ref[...], w_qkv_ref[...]).astype(BF).astype(F32)
    d_middle = (up_ref[...].astype(F32) + norm_back(middle, gain, d_second)).astype(BF)
    d_middle_ref[...] = d_middle
    d_heads = dot_nt(d_middle, w_out_ref[...])
    for hh in range(4):
        for jj in range(3):
            a = d_heads[(2 * jj) * 64 : (2 * jj + 1) * 64, hh * 128 : (hh + 1) * 128]
            b = d_heads[(2 * jj + 1) * 64 : (2 * jj + 2) * 64, hh * 128 : (hh + 1) * 128]
            cols = slice(jj * 128, (jj + 1) * 128)
            send_ref[2 * hh, :, cols] = jnp.where(lo64, a, swap(b)).astype(BF)
            send_ref[2 * hh + 1, :, cols] = jnp.where(lo64, swap(a), b).astype(BF)
    grads_ref[:, :1536] = outer(second_ref[...], d_qkv_ref[...])
    grads_ref[:, 1536:2048] = outer(heads_one_ref[...], d_middle)
    grads_ref[:, 2048:] = outer(heads_two_ref[...], up_ref[...])
    core = core_ref[0]
    keep_ref[...] = grads_ref[:, pl.ds(pl.multiple_of(core * 1280, 1280), 1280)]
    give_ref[...] = grads_ref[:, pl.ds(pl.multiple_of((1 - core) * 1280, 1280), 1280)]


def last_kernel(got_ref, w_ref, tokens_ref, gain_ref, d_middle_ref, out_ref, d_qkv_ref):
    lo = low_half(64)
    for hh in range(4):
        for jj in range(3):
            part = []
            for head in (2 * hh, 2 * hh + 1):
                for kind in range(3):
                    at = jj * 384 + kind * 128
                    part.append(got_ref[head, :, at : at + 128].astype(F32))
            for block in range(3):
                left, right = part[2 * block], part[2 * block + 1]
                at = hh * 384 + block * 128
                d_qkv_ref[(2 * jj) * 64 : (2 * jj + 1) * 64, at : at + 128] = jnp.where(
                    lo, left, swap(right)
                ).astype(BF)
                d_qkv_ref[(2 * jj + 1) * 64 : (2 * jj + 2) * 64, at : at + 128] = jnp.where(
                    lo, swap(left), right
                ).astype(BF)
    d_first = dot_nt(d_qkv_ref[...], w_ref[...]).astype(BF).astype(F32)
    x = tokens_ref[...].astype(F32)
    out_ref[...] = (
        d_middle_ref[...].astype(F32) + norm_back(x, gain_ref[...], d_first)
    ).astype(BF)


def column_kernel(first_ref, d_qkv_ref, out_ref):
    lo = low_half(64, 384)
    total = jnp.zeros((512, 384), F32)
    for s in range(8):
        rows = []
        for jj in range(3):
            block = d_qkv_ref[s * 64 : (s + 1) * 64, jj * 384 : (jj + 1) * 384].astype(F32)
            rows.append(jnp.where(lo, block, 0.0).astype(BF))
            rows.append(jnp.where(lo, 0.0, block).astype(BF))
        total = total + dot(first_ref[s], jnp.concatenate(rows, axis=0))
    low = low_half(512)
    sums = [total[:, i * 128 : (i + 1) * 128] for i in range(3)]
    sums = [x + swap(x) for x in sums]
    out_ref[:, 0:128] = jnp.where(low, sums[0], sums[1]).astype(BF)
    out_ref[:, 128:192] = sums[2][:, :HD].astype(BF)


def call(kernel, outs, args, scratch=(), flops=10**9, moved=4 * 10**6, exps=0, vmem=LARGE):
    return pl.pallas_call(
        kernel,
        out_shape=[jax.ShapeDtypeStruct(shape, dtype) for shape, dtype in outs],
        scratch_shapes=list(scratch),
        in_specs=[
            pl.BlockSpec(memory_space=pltpu.SMEM if x.dtype == jnp.int32 else pltpu.VMEM) for x in args
        ],
        compiler_params=pltpu.CompilerParams(vmem_limit_bytes=vmem),
        cost_estimate=pl.CostEstimate(flops=flops, bytes_accessed=moved, transcendentals=exps),
    )(*args)


def to_markers(x):
    lead = x.shape[:-2]
    k = len(lead) + 1
    n = lax.axis_size("marker")
    me = lax.axis_index("marker")
    x = x.reshape(*lead, 6, n, 8, 512)
    out = x
    for step in (4, 3, 5, 2, 6, 1, 7):
        give = lax.dynamic_slice_in_dim(x, lax.rem(me + step, n), 1, k)
        got = lax.ppermute(give, "marker", [(i, (i + step) % n) for i in range(n)])
        out = lax.dynamic_update_slice_in_dim(out, got, lax.rem(me + n - step, n), k)
    return out.reshape(*lead, 384, 512)


def swapped(x, bit):
    n = lax.axis_size("batch")
    return lax.ppermute(x, "batch", [(i, i ^ bit) for i in range(n)])


def halves(x, shift):
    width = x.shape[1] // 2
    mine = (lax.axis_index("batch") >> shift) & 1
    keep = lax.dynamic_slice_in_dim(x, mine * width, width, 1)
    give = lax.dynamic_slice_in_dim(x, (1 - mine) * width, width, 1)
    return keep, give


def halve(x, bit, shift):
    keep, give = halves(x, shift)
    return (keep.astype(F32) + swapped(give, bit).astype(F32)).astype(BF)


def on_device(
    tokens, gain_first, w_qkv_space, w_out_space, gain_second, w_qkv_marker, w_out_marker, upstream
):
    both = ("space", "marker")
    rows = ("marker", "space")
    mine = jnp.transpose(tokens[0], (1, 0, 2)).reshape(384, 512)
    up_mine = jnp.transpose(upstream[0], (1, 0, 2)).reshape(384, 512)
    gain_1 = gain_first.reshape(1, 512)
    gain_2 = gain_second.reshape(1, 512)

    first_t, qkv_send = call(
        project_kernel,
        [((512, 384), BF), ((8, 64, 1152), BF)],
        (mine, gain_1, w_qkv_space),
    )
    qkv_one = lax.all_to_all(qkv_send, "space", 0, 0, tiled=True).reshape(512, 1152)
    wide = to_markers(jnp.stack([mine, up_mine]))
    first_all = lax.all_gather(first_t, "space", axis=0, tiled=False)

    heads, inv = call(
        spatial_kernel, [((512, 384), BF), ((6, 512), F32)], (qkv_one,),
        flops=2 * 10**9, exps=6 * 512 * 512, vmem=SMALL,
    )
    got = lax.all_to_all(heads, both, 0, 0, tiled=True).reshape(8, 64, 384)

    up_all = wide[1]
    core = (lax.axis_index("batch") & 1).astype(jnp.int32).reshape(1)
    keep, give, d_middle, d_send = call(
        middle_kernel,
        [((512, 1280), BF), ((512, 1280), BF), ((384, 512), BF), ((8, 64, 384), BF)],
        (core, got, wide[0], up_all, w_out_space, gain_2, w_qkv_marker, w_out_marker),
        scratch=[
            pltpu.VMEM(shape, BF)
            for shape in ((512, 2560), (384, 512), (384, 512), (384, 1536), (384, 512), (384, 1536), (384, 512))
        ],
        flops=6 * 10**9, exps=8 * 384 * 384, vmem=LARGE,
    )
    d_heads = lax.all_to_all(d_send.reshape(512, 384), both, 0, 0, tiled=True)

    d_heads, first_all = lax.optimization_barrier((d_heads, first_all))
    d_qkv_one, = call(
        spatial_back_kernel, [((512, 1152), BF)], (qkv_one, heads, inv, d_heads),
        flops=10**6, moved=10**4, vmem=SMALL,
    )
    middle_all = lax.all_gather(d_middle, "marker", axis=0, tiled=False)
    share, give = halves((keep.astype(F32) + swapped(give, 1).astype(F32)).astype(BF), 1)
    give = swapped(give, 2)
    d_qkv_one, give = lax.optimization_barrier((d_qkv_one, give))
    d_back = lax.all_to_all(d_qkv_one, "space", 0, 0, tiled=True).reshape(8, 64, 1152)
    give, middle_all = lax.optimization_barrier((give, middle_all))
    share = (share.astype(F32) + give.astype(F32)).astype(BF)
    column, = call(column_kernel, [((512, 192), BF)], (first_all, d_qkv_one), flops=2 * 10**9)
    shares = jnp.concatenate([share, halve(column, 1, 0)], axis=1)
    shares, d_back = lax.optimization_barrier((shares, d_back))
    d_middle_mine = lax.dynamic_index_in_dim(
        middle_all.reshape(8, 6, 8, 8, 512), lax.axis_index("marker"), 2, keepdims=False
    )
    d_middle_mine = jnp.transpose(d_middle_mine, (1, 0, 2, 3)).reshape(384, 512)
    shares = lax.all_to_all(shares, rows, 0, 0, tiled=True).reshape(8, 8, 8, 736).astype(F32)
    column = jnp.sum(shares[..., 640:], axis=0).transpose(1, 0, 2).reshape(8, 768)
    share = jnp.sum(shares[..., :640], axis=(0, 1))
    share = jnp.concatenate([share, column], axis=1).astype(BF)
    share = lax.all_gather(share, "batch", axis=0, tiled=False)
    share = share.reshape(2, 2, 8, 1408).astype(F32)
    column = jnp.sum(share[..., 640:], axis=0).reshape(2, 8, 8, 96)
    column = column.transpose(1, 2, 0, 3).reshape(8, 1536)
    share = share[..., :640].transpose(2, 1, 0, 3).reshape(8, 2560)
    d_tokens, = call(
        last_kernel, [((384, 512), BF)], (d_back, w_qkv_space, mine, gain_1, d_middle_mine),
        scratch=[pltpu.VMEM((384, 1536), BF)], vmem=SMALL,
    )

    count = 1
    for axis in ("batch", "marker", "space"):
        count *= lax.axis_size(axis)
    factor = 1.0 / math.sqrt(count * 384)
    at = (lax.axis_index("marker") * 8 + lax.axis_index("space")) * 8

    own = [lax.dynamic_slice_in_dim(x, at, 8, 0) for x in (w_qkv_space, gain_first, w_qkv_marker, gain_second)]
    own = lax.optimization_barrier(own)

    def gain_grad(weight, gain, grad):
        return jnp.sum(weight.astype(F32) * grad, axis=1) / gain

    g_qkv_space = column * factor
    g_qkv_marker = share[:, :1536] * factor
    return (
        jnp.transpose(d_tokens.reshape(6, 64, 512), (1, 0, 2))[None],
        g_qkv_space,
        share[:, 1536:2048] * factor,
        gain_grad(own[0], own[1], g_qkv_space),
        g_qkv_marker,
        share[:, 2048:] * factor,
        gain_grad(own[2], own[3], g_qkv_marker),
    )


def solution(mesh):
    in_specs = (
        P("batch", "space", "marker", None),
        P(), P(), P(), P(), P(), P(),
        P("batch", "space", "marker", None),
    )
    shares = P(("marker", "space"), None)
    out_specs = (
        P("batch", "space", "marker", None),
        shares,
        shares,
        P(("marker", "space")),
        shares,
        shares,
        P(("marker", "space")),
    )
    return jax.shard_map(
        on_device, mesh=mesh, in_specs=in_specs, out_specs=out_specs, check_vma=False
    )
```

```python
import functools
import math

import jax
import jax.numpy as jnp
from jax import lax
from jax.experimental import pallas as pl
from jax.experimental.pallas import tpu as pltpu
from jax.sharding import PartitionSpec as P

HD = 64
EPS = 1e-06
BF = jnp.bfloat16
F32 = jnp.float32
LOG2E = math.log2(math.e)
SMALL = 24 * 1024 * 1024
LARGE = 56 * 1024 * 1024


def low_half(rows, width=128):
    return lax.broadcasted_iota(jnp.int32, (rows, width), 1) % 128 < HD


def swap(x):
    return pltpu.roll(x, HD, 1)


def dot(a, b):
    return jnp.dot(a, b, preferred_element_type=F32)


def dot_nt(a, b):
    return lax.dot_general(a, b, (((1,), (1,)), ((), ())), preferred_element_type=F32)


def outer(left, right):
    return lax.dot_general(
        left, right, (((0,), (0,)), ((), ())), preferred_element_type=F32
    ).astype(BF)


def half_mean(x, lo):
    first = jnp.sum(jnp.where(lo, x, 0.0), axis=-1, keepdims=True)
    second = jnp.sum(jnp.where(lo, 0.0, x), axis=-1, keepdims=True)
    return jnp.where(lo, first, second) * (1.0 / HD)


def half_scale(x, lo):
    return lax.rsqrt(half_mean(x * x, lo) + EPS)


def only_half(x, unit):
    own = x[unit * HD : (unit + 1) * HD]
    zero = jnp.zeros_like(own)
    return jnp.concatenate([own, zero] if unit == 0 else [zero, own], axis=0)


def row_scale(x):
    return lax.rsqrt(jnp.mean(x * x, axis=-1, keepdims=True) + EPS)


def norm_back(x, gain, cotangent):
    scale = row_scale(x)
    unit = x * scale
    pulled = cotangent * gain
    return scale * (pulled - unit * jnp.mean(pulled * unit, axis=-1, keepdims=True))


def scaled_pair(query, keys, lo):
    q_scale = half_scale(query, lo)
    k_scale = half_scale(keys, lo)
    return query * q_scale, q_scale, keys * k_scale, k_scale


def pair_back(d_qn, d_kn, qn, q_scale, kn, k_scale, lo):
    d_q = q_scale * (d_qn - qn * half_mean(d_qn * qn, lo))
    d_k = k_scale * (d_kn - kn * half_mean(d_kn * kn, lo))
    return d_q, d_k


def project_kernel(tokens_ref, gain_ref, w_ref, first_t_ref, send_ref):
    lo = low_half(64)
    x = tokens_ref[...].astype(F32)
    first = (x * row_scale(x) * gain_ref[...]).astype(BF)
    first_t_ref[...] = first.astype(F32).T.astype(BF)
    for hh in range(4):
        wide = dot(first, w_ref[:, hh * 384 : (hh + 1) * 384])
        for jj in range(3):
            a = wide[(2 * jj) * 64 : (2 * jj + 1) * 64]
            b = wide[(2 * jj + 1) * 64 : (2 * jj + 2) * 64]
            for block in range(3):
                ba = a[:, block * 128 : (block + 1) * 128]
                bb = b[:, block * 128 : (block + 1) * 128]
                left = jnp.where(lo, ba, swap(bb)).astype(BF)
                right = jnp.where(lo, swap(ba), bb).astype(BF)
                for half, value in ((0, left), (1, right)):
                    part = 2 * block + half
                    head, kind = 2 * hh + part // 3, part % 3
                    at = jj * 384 + kind * 128
                    send_ref[head, :, at : at + 128] = value


def spatial_kernel(qkv_ref, heads_ref, inv_ref):
    length = qkv_ref.shape[0]
    lo = low_half(length)
    step = 512
    for jj in range(3):
        at = jj * 384
        query = qkv_ref[:, at : at + 128].astype(F32)
        keys = qkv_ref[:, at + 128 : at + 256].astype(F32)
        values = qkv_ref[:, at + 256 : at + 384].astype(F32)
        qn, _, kn, _ = scaled_pair(query, keys, lo)
        q_t = (qn * (LOG2E / 8.0)).T.astype(BF)
        kb = kn.astype(BF)
        v_t = values.T.astype(BF)
        out = []
        for unit in range(2):
            q_own = only_half(q_t, unit)
            cols = []
            for start in range(0, length, step):
                e = jnp.exp2(dot(kb, q_own[:, start : start + step]))
                inv = 1.0 / jnp.sum(e, axis=0, keepdims=True)
                inv_ref[2 * jj + unit : 2 * jj + unit + 1, start : start + step] = inv
                cols.append(dot(v_t[unit * HD : (unit + 1) * HD], e.astype(BF)) * inv)
            out.append(jnp.concatenate(cols, axis=1))
        heads_ref[:, jj * 128 : (jj + 1) * 128] = jnp.concatenate(out, axis=0).T.astype(BF)


def spatial_back_kernel(qkv_ref, heads_ref, inv_ref, d_heads_ref, d_qkv_ref):
    length = qkv_ref.shape[0]
    lo = low_half(length)
    step = 512
    for jj in range(3):
        at = jj * 384
        query = qkv_ref[:, at : at + 128].astype(F32)
        keys = qkv_ref[:, at + 128 : at + 256].astype(F32)
        vb = qkv_ref[:, at + 256 : at + 384]
        qn, q_scale, kn, k_scale = scaled_pair(query, keys, lo)
        qs = qn * (LOG2E / 8.0)
        q_t = qs.T.astype(BF)
        qb = qs.astype(BF)
        kb = kn.astype(BF)
        k_t = kn.T.astype(BF)
        o_t = heads_ref[:, jj * 128 : (jj + 1) * 128].astype(F32).T
        g_t = d_heads_ref[:, jj * 128 : (jj + 1) * 128].astype(F32).T
        scaled, drops = [], []
        for unit in range(2):
            rows = slice(unit * HD, (unit + 1) * HD)
            own = g_t[rows] * inv_ref[2 * jj + unit : 2 * jj + unit + 1, :]
            scaled.append(own)
            drops.append(jnp.sum(own * o_t[rows], axis=0, keepdims=True))
        g_scaled = jnp.concatenate(scaled, axis=0)
        gb = g_scaled.T.astype(BF)
        g_scaled = g_scaled.astype(BF)
        d_q, d_k, d_v = [], [], []
        for unit in range(2):
            q_own = only_half(q_t, unit)
            g_own = only_half(g_scaled, unit)
            cols, dk, dv = [], 0.0, 0.0
            for start in range(0, length, step):
                part = slice(start, start + step)
                e = jnp.exp2(dot(kb, q_own[:, part]))
                ds = (e * (dot(vb, g_own[:, part]) - drops[unit][:, part])).astype(BF)
                cols.append(dot(k_t[unit * HD : (unit + 1) * HD], ds))
                dk = dk + dot(ds, qb[part])
                dv = dv + dot(e.astype(BF), gb[part])
            d_q.append(jnp.concatenate(cols, axis=1))
            d_k.append(dk)
            d_v.append(dv)
        d_qn = jnp.concatenate(d_q, axis=0).T * (1.0 / 8.0)
        d_kn = jnp.where(lo, d_k[0], d_k[1]) * (1.0 / LOG2E)
        dq, dk = pair_back(d_qn, d_kn, qn, q_scale, kn, k_scale, lo)
        d_qkv_ref[:, at : at + 128] = dq.astype(BF)
        d_qkv_ref[:, at + 128 : at + 256] = dk.astype(BF)
        d_qkv_ref[:, at + 256 : at + 384] = jnp.where(lo, d_v[0], d_v[1]).astype(BF)


def middle_kernel(
    core_ref, got_ref, tokens_ref, up_ref, w_out_ref, gain_ref, w_qkv_ref, w_last_ref,
    keep_ref, give_ref, d_middle_ref, send_ref,
    grads_ref, heads_one_ref, second_ref, d_qkv_ref, heads_two_ref, qkv_ref, d_two_ref,
):
    lo64 = low_half(64)
    for hh in range(4):
        for jj in range(3):
            a = got_ref[2 * hh, :, jj * 128 : (jj + 1) * 128].astype(F32)
            b = got_ref[2 * hh + 1, :, jj * 128 : (jj + 1) * 128].astype(F32)
            cols = slice(hh * 128, (hh + 1) * 128)
            heads_one_ref[(2 * jj) * 64 : (2 * jj + 1) * 64, cols] = jnp.where(lo64, a, swap(b)).astype(BF)
            heads_one_ref[(2 * jj + 1) * 64 : (2 * jj + 2) * 64, cols] = jnp.where(lo64, swap(a), b).astype(BF)
    middle = tokens_ref[...].astype(F32) + dot(heads_one_ref[...], w_out_ref[...])
    middle = middle.astype(BF).astype(F32)
    gain = gain_ref[...]
    second = (middle * row_scale(middle) * gain).astype(BF)
    second_ref[...] = second
    qkv_ref[...] = dot(second, w_qkv_ref[...]).astype(BF)
    d_two_ref[...] = dot_nt(up_ref[...], w_last_ref[...]).astype(BF)

    length = qkv_ref.shape[0]
    lo = low_half(length)
    same = (
        lax.broadcasted_iota(jnp.int32, (length, length), 0) % 8
        == lax.broadcasted_iota(jnp.int32, (length, length), 1) % 8
    )
    for hh in range(4):
        at = hh * 384
        b0 = qkv_ref[:, at : at + 128].astype(F32)
        b1 = qkv_ref[:, at + 128 : at + 256].astype(F32)
        b2 = qkv_ref[:, at + 256 : at + 384].astype(F32)
        query = jnp.where(lo, b0, b1)
        keys = swap(jnp.where(lo, b2, b0))
        values = jnp.where(lo, b1, b2)
        qn, q_scale, kn, k_scale = scaled_pair(query, keys, lo)
        qs = qn * (LOG2E / 8.0)
        q_t = qs.T.astype(BF)
        qb = qs.astype(BF)
        kb = kn.astype(BF)
        k_t = kn.T.astype(BF)
        vb = values.astype(BF)
        v_t = values.T.astype(BF)
        g_t = d_two_ref[:, hh * 128 : (hh + 1) * 128].astype(F32).T
        o_t, d_q, d_k, d_v = [], [], [], []
        for unit in range(2):
            rows = slice(unit * HD, (unit + 1) * HD)
            e = jnp.where(same, jnp.exp2(dot(kb, only_half(q_t, unit))), 0.0)
            inv = 1.0 / jnp.sum(e, axis=0, keepdims=True)
            eb = e.astype(BF)
            o = dot(v_t[rows], eb) * inv
            own = g_t[rows] * inv
            drop = jnp.sum(own * o, axis=0, keepdims=True)
            zero = jnp.zeros_like(own)
            g_own = jnp.concatenate([own, zero] if unit == 0 else [zero, own], axis=0)
            gb = g_own.T.astype(BF)
            ds = (e * (dot(vb, g_own.astype(BF)) - drop)).astype(BF)
            o_t.append(o)
            d_q.append(dot(k_t[rows], ds))
            d_k.append(dot(ds, qb))
            d_v.append(dot(eb, gb))
        heads_two_ref[:, hh * 128 : (hh + 1) * 128] = jnp.concatenate(o_t, axis=0).T.astype(BF)
        d_qn = jnp.concatenate(d_q, axis=0).T * (1.0 / 8.0)
        d_kn = jnp.where(lo, d_k[0], d_k[1]) * (1.0 / LOG2E)
        dq, dk = pair_back(d_qn, d_kn, qn, q_scale, kn, k_scale, lo)
        dv = jnp.where(lo, d_v[0], d_v[1])
        dk = swap(dk)
        d_qkv_ref[:, at : at + 128] = jnp.where(lo, dq, dk).astype(BF)
        d_qkv_ref[:, at + 128 : at + 256] = jnp.where(lo, dv, dq).astype(BF)
        d_qkv_ref[:, at + 256 : at + 384] = jnp.where(lo, dk, dv).astype(BF)

    d_second = dot_nt(d_qkv_ref[...], w_qkv_ref[...]).astype(BF).astype(F32)
    d_middle = (up_ref[...].astype(F32) + norm_back(middle, gain, d_second)).astype(BF)
    d_middle_ref[...] = d_middle
    d_heads = dot_nt(d_middle, w_out_ref[...])
    for hh in range(4):
        for jj in range(3):
            a = d_heads[(2 * jj) * 64 : (2 * jj + 1) * 64, hh * 128 : (hh + 1) * 128]
            b = d_heads[(2 * jj + 1) * 64 : (2 * jj + 2) * 64, hh * 128 : (hh + 1) * 128]
            cols = slice(jj * 128, (jj + 1) * 128)
            send_ref[2 * hh, :, cols] = jnp.where(lo64, a, swap(b)).astype(BF)
            send_ref[2 * hh + 1, :, cols] = jnp.where(lo64, swap(a), b).astype(BF)
    grads_ref[:, :1536] = outer(second_ref[...], d_qkv_ref[...])
    grads_ref[:, 1536:2048] = outer(heads_one_ref[...], d_middle)
    grads_ref[:, 2048:] = outer(heads_two_ref[...], up_ref[...])
    core = core_ref[0]
    keep_ref[...] = grads_ref[:, pl.ds(pl.multiple_of(core * 1280, 1280), 1280)]
    give_ref[...] = grads_ref[:, pl.ds(pl.multiple_of((1 - core) * 1280, 1280), 1280)]


def last_kernel(got_ref, w_ref, tokens_ref, gain_ref, d_middle_ref, out_ref, d_qkv_ref):
    lo = low_half(64)
    for hh in range(4):
        for jj in range(3):
            part = []
            for head in (2 * hh, 2 * hh + 1):
                for kind in range(3):
                    at = jj * 384 + kind * 128
                    part.append(got_ref[head, :, at : at + 128].astype(F32))
            for block in range(3):
                left, right = part[2 * block], part[2 * block + 1]
                at = hh * 384 + block * 128
                d_qkv_ref[(2 * jj) * 64 : (2 * jj + 1) * 64, at : at + 128] = jnp.where(
                    lo, left, swap(right)
                ).astype(BF)
                d_qkv_ref[(2 * jj + 1) * 64 : (2 * jj + 2) * 64, at : at + 128] = jnp.where(
                    lo, swap(left), right
                ).astype(BF)
    d_first = dot_nt(d_qkv_ref[...], w_ref[...]).astype(BF).astype(F32)
    x = tokens_ref[...].astype(F32)
    out_ref[...] = (
        d_middle_ref[...].astype(F32) + norm_back(x, gain_ref[...], d_first)
    ).astype(BF)


def column_kernel(first_ref, d_qkv_ref, out_ref):
    lo = low_half(64, 384)
    total = jnp.zeros((512, 384), F32)
    for s in range(8):
        rows = []
        for jj in range(3):
            block = d_qkv_ref[s * 64 : (s + 1) * 64, jj * 384 : (jj + 1) * 384].astype(F32)
            rows.append(jnp.where(lo, block, 0.0).astype(BF))
            rows.append(jnp.where(lo, 0.0, block).astype(BF))
        total = total + dot(first_ref[s], jnp.concatenate(rows, axis=0))
    low = low_half(512)
    sums = [total[:, i * 128 : (i + 1) * 128] for i in range(3)]
    sums = [x + swap(x) for x in sums]
    out_ref[:, 0:128] = jnp.where(low, sums[0], sums[1]).astype(BF)
    out_ref[:, 128:192] = sums[2][:, :HD].astype(BF)


def call(kernel, outs, args, scratch=(), flops=10**9, moved=4 * 10**6, exps=0, vmem=LARGE):
    return pl.pallas_call(
        kernel,
        out_shape=[jax.ShapeDtypeStruct(shape, dtype) for shape, dtype in outs],
        scratch_shapes=list(scratch),
        in_specs=[
            pl.BlockSpec(memory_space=pltpu.SMEM if x.dtype == jnp.int32 else pltpu.VMEM) for x in args
        ],
        compiler_params=pltpu.CompilerParams(vmem_limit_bytes=vmem),
        cost_estimate=pl.CostEstimate(flops=flops, bytes_accessed=moved, transcendentals=exps),
    )(*args)


def to_markers(x):
    lead = x.shape[:-2]
    k = len(lead) + 1
    n = lax.axis_size("marker")
    me = lax.axis_index("marker")
    x = x.reshape(*lead, 6, n, 8, 512)
    out = x
    for step in (1, 7, 2, 6, 3, 5, 4):
        give = lax.dynamic_slice_in_dim(x, lax.rem(me + step, n), 1, k)
        got = lax.ppermute(give, "marker", [(i, (i + step) % n) for i in range(n)])
        out = lax.dynamic_update_slice_in_dim(out, got, lax.rem(me + n - step, n), k)
    return out.reshape(*lead, 384, 512)


def swapped(x, bit):
    n = lax.axis_size("batch")
    return lax.ppermute(x, "batch", [(i, i ^ bit) for i in range(n)])


def halves(x, shift):
    width = x.shape[1] // 2
    mine = (lax.axis_index("batch") >> shift) & 1
    keep = lax.dynamic_slice_in_dim(x, mine * width, width, 1)
    give = lax.dynamic_slice_in_dim(x, (1 - mine) * width, width, 1)
    return keep, give


def halve(x, bit, shift):
    keep, give = halves(x, shift)
    return (keep.astype(F32) + swapped(give, bit).astype(F32)).astype(BF)


def on_device(
    tokens, gain_first, w_qkv_space, w_out_space, gain_second, w_qkv_marker, w_out_marker, upstream
):
    both = ("space", "marker")
    rows = ("marker", "space")
    mine = jnp.transpose(tokens[0], (1, 0, 2)).reshape(384, 512)
    up_mine = jnp.transpose(upstream[0], (1, 0, 2)).reshape(384, 512)
    gain_1 = gain_first.reshape(1, 512)
    gain_2 = gain_second.reshape(1, 512)

    first_t, qkv_send = call(
        project_kernel,
        [((512, 384), BF), ((8, 64, 1152), BF)],
        (mine, gain_1, w_qkv_space),
    )
    qkv_one = lax.all_to_all(qkv_send, "space", 0, 0, tiled=True).reshape(512, 1152)
    wide = to_markers(jnp.stack([mine, up_mine]))
    first_all = lax.all_gather(first_t, "space", axis=0, tiled=False)

    heads, inv = call(
        spatial_kernel, [((512, 384), BF), ((6, 512), F32)], (qkv_one,),
        flops=2 * 10**9, exps=6 * 512 * 512, vmem=SMALL,
    )
    got = lax.all_to_all(heads, both, 0, 0, tiled=True).reshape(8, 64, 384)

    up_all = wide[1]
    core = (lax.axis_index("batch") & 1).astype(jnp.int32).reshape(1)
    keep, give, d_middle, d_send = call(
        middle_kernel,
        [((512, 1280), BF), ((512, 1280), BF), ((384, 512), BF), ((8, 64, 384), BF)],
        (core, got, wide[0], up_all, w_out_space, gain_2, w_qkv_marker, w_out_marker),
        scratch=[
            pltpu.VMEM(shape, BF)
            for shape in ((512, 2560), (384, 512), (384, 512), (384, 1536), (384, 512), (384, 1536), (384, 512))
        ],
        flops=6 * 10**9, exps=8 * 384 * 384, vmem=LARGE,
    )
    d_heads = lax.all_to_all(d_send.reshape(512, 384), both, 0, 0, tiled=True)

    d_heads, first_all = lax.optimization_barrier((d_heads, first_all))
    d_qkv_one, = call(
        spatial_back_kernel, [((512, 1152), BF)], (qkv_one, heads, inv, d_heads),
        flops=10**6, moved=10**4, vmem=SMALL,
    )
    middle_all = lax.all_gather(d_middle, "marker", axis=0, tiled=False)
    share, give = halves((keep.astype(F32) + swapped(give, 1).astype(F32)).astype(BF), 1)
    give = swapped(give, 2)
    d_qkv_one, give = lax.optimization_barrier((d_qkv_one, give))
    d_back = lax.all_to_all(d_qkv_one, "space", 0, 0, tiled=True).reshape(8, 64, 1152)
    give, middle_all = lax.optimization_barrier((give, middle_all))
    share = (share.astype(F32) + give.astype(F32)).astype(BF)
    column, = call(column_kernel, [((512, 192), BF)], (first_all, d_qkv_one), flops=2 * 10**9)
    shares = jnp.concatenate([share, halve(column, 1, 0)], axis=1)
    shares, d_back = lax.optimization_barrier((shares, d_back))
    d_middle_mine = lax.dynamic_index_in_dim(
        middle_all.reshape(8, 6, 8, 8, 512), lax.axis_index("marker"), 2, keepdims=False
    )
    d_middle_mine = jnp.transpose(d_middle_mine, (1, 0, 2, 3)).reshape(384, 512)
    shares = lax.all_to_all(shares, rows, 0, 0, tiled=True).reshape(8, 8, 8, 736).astype(F32)
    column = jnp.sum(shares[..., 640:], axis=0).transpose(1, 0, 2).reshape(8, 768)
    share = jnp.sum(shares[..., :640], axis=(0, 1))
    share = jnp.concatenate([share, column], axis=1).astype(BF)
    share = lax.all_gather(share, "batch", axis=0, tiled=False)
    share = share.reshape(2, 2, 8, 1408).astype(F32)
    column = jnp.sum(share[..., 640:], axis=0).reshape(2, 8, 8, 96)
    column = column.transpose(1, 2, 0, 3).reshape(8, 1536)
    share = share[..., :640].transpose(2, 1, 0, 3).reshape(8, 2560)
    d_tokens, = call(
        last_kernel, [((384, 512), BF)], (d_back, w_qkv_space, mine, gain_1, d_middle_mine),
        scratch=[pltpu.VMEM((384, 1536), BF)], vmem=SMALL,
    )

    count = 1
    for axis in ("batch", "marker", "space"):
        count *= lax.axis_size(axis)
    factor = 1.0 / math.sqrt(count * 384)
    at = (lax.axis_index("marker") * 8 + lax.axis_index("space")) * 8

    own = [lax.dynamic_slice_in_dim(x, at, 8, 0) for x in (w_qkv_space, gain_first, w_qkv_marker, gain_second)]
    own = lax.optimization_barrier(own)

    def gain_grad(weight, gain, grad):
        return jnp.sum(weight.astype(F32) * grad, axis=1) / gain

    g_qkv_space = column * factor
    g_qkv_marker = share[:, :1536] * factor
    return (
        jnp.transpose(d_tokens.reshape(6, 64, 512), (1, 0, 2))[None],
        g_qkv_space,
        share[:, 1536:2048] * factor,
        gain_grad(own[0], own[1], g_qkv_space),
        g_qkv_marker,
        share[:, 2048:] * factor,
        gain_grad(own[2], own[3], g_qkv_marker),
    )


def solution(mesh):
    in_specs = (
        P("batch", "space", "marker", None),
        P(), P(), P(), P(), P(), P(),
        P("batch", "space", "marker", None),
    )
    shares = P(("marker", "space"), None)
    out_specs = (
        P("batch", "space", "marker", None),
        shares,
        shares,
        P(("marker", "space")),
        shares,
        shares,
        P(("marker", "space")),
    )
    return jax.shard_map(
        on_device, mesh=mesh, in_specs=in_specs, out_specs=out_specs, check_vma=False
    )
```
